512 devices in a mesh: seq: 128 (over y_hi, x, z), mp: 4 (over y_lo, core).
Axes of the slice: x: 4, y: 4 (y_hi: 2, y_lo: 2; y = y_hi * 2 + y_lo), z: 16, core: 2. Of those that a mesh axis runs over, the one named last changes fastest.
Arguments:
- queries: bfloat16 [16384, 1200], P('seq', 'mp'), may hold values from -8 to 8
- keys: bfloat16 [16384, 1200], P('seq', 'mp'), may hold values from -8 to 8
- values: bfloat16 [16384, 1200], P('seq', 'mp'), may hold values from -6 to 6
- weight_out: bfloat16 [2560, 1200], P('mp'), may hold values from -0.1875 to 0.1875
- grad_out: bfloat16 [16384, 2560], P('seq', 'mp'), may hold values from -24 to 24
Outputs:
- layer_out: bfloat16 [16384, 2560], P('seq', 'mp')
- grad_queries: bfloat16 [16384, 1200], P('seq', 'mp')
- grad_keys: bfloat16 [16384, 1200], P('seq', 'mp')
- grad_values: bfloat16 [16384, 1200], P('seq', 'mp')
- grad_weight: float32 [2560, 1200], P(('mp', 'seq'))
The draws below stay inside these ranges and needn't reach their ends.
All inputs are finite; a program needn't handle non-finite values.
Results may differ from the reference program's by a relative error of at most 0.02.
Values may be sent and summed in bfloat16 or wider, within the bound.
A program may use at most 64 MiB of HBM per device.

```python
import jax
import jax.numpy as jnp
from jax import lax

H = 8
HD = 150
OUTW = 2560
BLOCK = 1024
TOKENS = 16384
N_MP = 4


def draw_queries(key, part):
    key = jax.random.fold_in(key, 11)
    own = jnp.clip(jax.random.normal(key, (TOKENS, H * HD), jnp.float32), -4.0, 4.0)
    return own.astype(jnp.bfloat16)


def draw_keys(key, part):
    key = jax.random.fold_in(key, 23)
    own = jnp.clip(jax.random.normal(key, (TOKENS, H * HD), jnp.float32), -4.0, 4.0)
    return own.astype(jnp.bfloat16)


def spiked(result, own_key, source, target, parts, factor):
    def block_of(dim):
        return (jnp.arange(result.shape[dim]) // (result.shape[dim] // parts)).reshape((-1,) + (1,) * (result.ndim - 1 - dim))

    one_side = jax.random.permutation(own_key, parts)[block_of(target)]
    second = (block_of(target) + parts // 2) % parts
    return jnp.where((block_of(source) == one_side) | (block_of(source) == second), factor * result, result)


def steps_of(stream_key, extent, pieces, smallest, high):
    def one(dim, parts):
        steps = jax.random.uniform(jax.random.fold_in(jax.random.fold_in(stream_key, 6), dim), (parts,), jnp.float32, smallest / len(pieces), high / len(pieces))
        return jnp.repeat(jnp.exp(steps), extent[dim] // parts).reshape((-1,) + (1,) * (len(extent) - dim - 1))

    loudness = one(*pieces[0])
    for cut in pieces[1:]:
        loudness = loudness * one(*cut)
    return loudness


def centred(stream_key, extent, spread, limit, shards=(), kind=jnp.bfloat16):
    result = jax.random.normal(stream_key, extent, jnp.float32) * spread
    if len(shards) > 0:
        result = steps_of(stream_key, extent, shards, -0.22, 0.18) * result
    return jnp.clip(result, min=-limit, max=limit).astype(kind)


def noise_with(stream_key, shape, scale, limit, cuts, heavy, dtype=jnp.bfloat16):
    drawn = scale * jax.random.normal(stream_key, shape, jnp.float32)
    if cuts:
        drawn = drawn * steps_of(stream_key, shape, cuts, -0.22, 0.18)
    return jnp.clip(spiked(drawn, jax.random.fold_in(stream_key, 3), *heavy), -limit, limit).astype(dtype)


def setup_inputs(seed: int = 0) -> dict:
    seeds = jax.random.split(jax.random.key(seed), 6)
    queries = draw_queries(jax.random.fold_in(seeds[5], 71), 0)
    keys = draw_keys(jax.random.fold_in(seeds[5], 71), 0)
    values = centred(seeds[2], (TOKENS, H * HD), 1.0, 6.0, ((0, 128), (1, 4)))
    weight_out = centred(seeds[3], (OUTW, H * HD), (H * HD) ** -0.5, 0.1875, ((0, 4),))
    grad_out = noise_with(seeds[4], (TOKENS, OUTW), 1.0, 24.0, ((0, 128), (1, 4)), (0, 1, 128, 5.5))
    return dict(queries=queries, keys=keys, values=values, weight_out=weight_out, grad_out=grad_out)


NEG = -1.0e30


def rounded(x):
    return lax.optimization_barrier(x.astype(jnp.bfloat16)).astype(jnp.float32)


def reference(queries, keys, values, weight_out, grad_out):
    rows = TOKENS // BLOCK
    width = H * HD
    scale = HD ** -0.5
    qfull = queries.reshape(rows, BLOCK, H, HD).astype(jnp.float32)
    kfull = keys.reshape(rows, BLOCK, H, HD).astype(jnp.float32)
    vfull = values.reshape(rows, BLOCK, H, HD).astype(jnp.float32)
    causal = (jnp.arange(BLOCK)[None, :] <= jnp.arange(BLOCK)[:, None])[:, None, :]
    row_ids = jnp.arange(rows)

    def scores_for(r):
        qf = qfull[r]
        rs = jnp.einsum("chd,khd->chk", qf, kfull[r]) * scale
        cs = jnp.einsum("chd,schd->chs", qf, kfull) * scale
        cmask = (row_ids < r)[None, None, :]
        return qf, rs, cs, cmask

    def forward_row(r):
        qf, rs, cs, cmask = scores_for(r)
        rmax = jnp.max(jnp.where(causal, rs, NEG), axis=2)
        rprob = jnp.where(causal, jnp.exp(rs - rmax[..., None]), 0.0)
        rtot = jnp.sum(rprob, axis=2)
        racc = jnp.einsum("chk,khd->chd", rounded(rprob), vfull[r])
        cmax = jnp.max(jnp.where(cmask, cs, NEG), axis=2)
        cprob = jnp.where(cmask, jnp.exp(cs - cmax[..., None]), 0.0)
        ctot = jnp.sum(cprob, axis=2)
        cacc = jnp.einsum("chs,schd->chd", rounded(cprob), vfull)
        top = jnp.maximum(rmax, cmax)
        near = jnp.exp(rmax - top)
        far = jnp.exp(cmax - top)
        total = rtot * near + ctot * far
        out = (racc * near[..., None] + cacc * far[..., None]) / total[..., None]
        return out.astype(jnp.bfloat16), top + jnp.log(total)

    attn4, lse4 = lax.map(forward_row, row_ids)
    attn = attn4.reshape(TOKENS, width)
    layer_out = jnp.dot(attn, weight_out.T, preferred_element_type=jnp.float32).astype(jnp.bfloat16)
    grad_weight = jnp.dot(grad_out.T, attn, preferred_element_type=jnp.float32)
    per = OUTW // N_MP
    dsum = jnp.zeros((TOKENS, width), jnp.float32)
    for group in range(N_MP):
        part = jnp.dot(grad_out[:, group * per:(group + 1) * per], weight_out[group * per:(group + 1) * per], preferred_element_type=jnp.float32)
        dsum = dsum + rounded(part)
    dattn4 = dsum.astype(jnp.bfloat16).reshape(rows, BLOCK, H, HD)
    delta4 = jnp.sum(dattn4.astype(jnp.float32) * attn4.astype(jnp.float32), axis=3)

    def back_row(carry, r):
        gk_all, gv_all = carry
        qf, rs, cs, cmask = scores_for(r)
        dout = dattn4[r].astype(jnp.float32)
        lse = lse4[r][..., None]
        dl = delta4[r][..., None]
        rprob = jnp.where(causal, jnp.exp(rs - lse), 0.0)
        rdp = jnp.einsum("chd,khd->chk", dout, vfull[r])
        rds = rounded(rprob * (rdp - dl))
        cprob = jnp.where(cmask, jnp.exp(cs - lse), 0.0)
        cdp = jnp.einsum("chd,schd->chs", dout, vfull)
        cds = rounded(cprob * (cdp - dl))
        gq = scale * jnp.einsum("chk,khd->chd", rds, kfull[r]) + scale * jnp.einsum("chs,schd->chd", cds, kfull)
        rk = scale * jnp.einsum("chk,chd->khd", rds, qf)
        rv = jnp.einsum("chk,chd->khd", rounded(rprob), dout)
        ck = scale * jnp.einsum("chs,chd->schd", cds, qf)
        cv = jnp.einsum("chs,chd->schd", rounded(cprob), dout)
        gk_all = (gk_all + ck).at[r].add(rk)
        gv_all = (gv_all + cv).at[r].add(rv)
        return (gk_all, gv_all), gq

    start = (jnp.zeros((rows, BLOCK, H, HD), jnp.float32), jnp.zeros((rows, BLOCK, H, HD), jnp.float32))
    (gk_all, gv_all), gq_all = lax.scan(back_row, start, row_ids)
    grad_queries = gq_all.reshape(TOKENS, width).astype(jnp.bfloat16)
    grad_keys = gk_all.reshape(TOKENS, width).astype(jnp.bfloat16)
    grad_values = gv_all.reshape(TOKENS, width).astype(jnp.bfloat16)
    return (layer_out, grad_queries, grad_keys, grad_values, grad_weight)
```

```python
import jax
import jax.numpy as jnp
from jax import lax
from jax.experimental import pallas as pl
from jax.experimental.pallas import tpu as pltpu
from jax.sharding import PartitionSpec as P

MESH = pl.DeviceIdType.MESH
HD = 150
W = 300
WP = 384
TOK = 128
NEG = -1e30
SCALE = HD ** (-0.5)
F32 = jnp.float32
BF16 = jnp.bfloat16


def nn(a, b):
    return jnp.dot(a, b, preferred_element_type=F32)


def nt(a, b):
    return lax.dot_general(a, b, (((1,), (1,)), ((), ())), preferred_element_type=F32)


def tn(a, b):
    return lax.dot_general(a, b, (((0,), (0,)), ((), ())), preferred_element_type=F32)


def iota(shape, dim):
    return lax.broadcasted_iota(jnp.int32, shape, dim)


def head_pair(x):
    lane = iota(x.shape, 1)
    a = jnp.where(lane < HD, x, 0.0)
    b = jnp.where((lane >= HD) & (lane < W), x, 0.0)
    return jnp.concatenate([a, b], axis=0).astype(BF16)


def pick(x2):
    n = x2.shape[0] // 2
    lane = iota((n, WP), 1)
    return jnp.where(lane < HD, x2[:n], x2[n:])


def padded(x):
    x = x.astype(F32)
    return jnp.concatenate([x, jnp.zeros((x.shape[0], WP - x.shape[1]), F32)], axis=1)


def kernel(
    q_ref, k_ref, v_ref, w_ref, go_ref,
    lay_ref, gq_ref, gk_ref, gv_ref, gw_ref,
    kv, q2, d2, acc2, m_ref, l_ref, gq2, own,
    part, mpin, colx, colin, cold, coldin, colo, coloin, coli, coliin, colg, colgin,
    att, goh, goin, gwin, gz1, z1in, gz2, z2in, gfx, fxin, rbs, rbin, info_t, dat,
    row_s, row_r, rb_s, rb_r, mp_s, mp_r, ag_s, ag_r,
    ca_s, ca_r, cd_s, cd_r, co_s, co_r, ci_s, ci_r, cg_s, cg_r,
    go_s, go_r, gw_s, gw_r, z1_s, z1_r, z2_s, z2_r, fx_s, fx_r,
):
    s = lax.axis_index("seq")
    m = lax.axis_index("mp")
    r, cg = s // 8, s % 8
    yh, x, z = s // 64, (s // 16) % 4, s % 16
    zq, zr = z // 4, z % 4
    g = yh * 4 + x

    def copy(src, dst, ss, rs, dev):
        return pltpu.make_async_remote_copy(
            src_ref=src, dst_ref=dst, send_sem=ss, recv_sem=rs, device_id=dev, device_id_type=MESH
        )

    def col_dev(rr):
        return (rr * 8 + cg, m)

    def g_dev(gg):
        return ((gg // 4) * 64 + (gg % 4) * 16 + z, m)

    def z_dev(zz):
        return (yh * 64 + x * 16 + zz, m)

    def x_dev(xx):
        return (yh * 64 + xx * 16 + z, m)

    bar = pltpu.get_barrier_semaphore()

    def greet(dev):
        pl.semaphore_signal(bar, inc=1, device_id=dev, device_id_type=MESH)

    def each(n, f):
        lax.fori_loop(1, n, lambda i, c: (f(i), c)[1], 0)

    each(16, lambda i: greet(col_dev((r + i) % 16)))
    each(4, lambda i: greet((s, (m + i) % 4)))
    each(4, lambda i: greet(z_dev(zq * 4 + (zr + i) % 4)))
    each(4, lambda i: greet(z_dev(((zq + i) % 4) * 4 + zr)))

    @pl.when(cg > 0)
    def _():
        greet((s - 1, m))

    @pl.when(cg < 7)
    def _():
        greet((s + 1, m))

    q32 = padded(q_ref[...])
    k32 = padded(k_ref[...])
    v32 = padded(v_ref[...])
    kv[0, 0] = k32.astype(BF16)
    kv[0, 1] = v32.astype(BF16)
    q2[...] = head_pair(q32)
    blocks = [t.reshape(16, 8, WP) for t in (q32, k32, v32, jnp.zeros_like(q32))]
    colx[...] = jnp.concatenate(blocks, axis=1).astype(BF16)
    pg = nn(go_ref[...], w_ref[...])
    for i in range(4):
        part[i] = padded(pg[:, W * i : W * i + W]).astype(BF16)
    go32 = go_ref[...].astype(F32)
    zer = jnp.zeros((TOK, WP - 320), F32)
    goh[0] = jnp.concatenate([go32[:, :320], zer], axis=1).astype(BF16)
    goh[1] = jnp.concatenate([go32[:, 320:], zer], axis=1).astype(BF16)

    links = (cg > 0).astype(jnp.int32) + (cg < 7).astype(jnp.int32)
    pl.semaphore_wait(bar, 15 + 3 + 3 + 3 + links)

    def row_copy(t, i):
        return copy(kv.at[t, i], kv.at[t + 1, i], row_s.at[t, i], row_r.at[t + 1, i], (s + 1, m))

    def row_send(t):
        @pl.when(cg < 7)
        def _():
            row_copy(t, 0).start()
            row_copy(t, 1).start()

    row_send(0)

    def mp_copy(i):
        o = (m + i) % 4
        return copy(part.at[o], mpin.at[m], mp_s.at[o], mp_r.at[m], (s, o))

    each(4, lambda i: mp_copy(i).start())

    def col_send(src, dst, ss, rs, i):
        o = (r + i) % 16
        return copy(src.at[o], dst.at[r], ss.at[o], rs.at[r], col_dev(o))

    def col_wait(src, dst, ss, rs, i):
        o = (r + i) % 16
        copy(src.at[o], dst.at[o], ss.at[o], rs.at[o], col_dev(o)).wait_recv()

    each(16, lambda i: col_send(colx, colin, ca_s, ca_r, i).start())
    colin[r] = colx[r]

    def go_copy(i):
        o = (g + i) % 8
        return copy(goh.at[o // 4], goin.at[g], go_s.at[o], go_r.at[g], g_dev(o))

    each(8, lambda i: go_copy(i).start())
    goin[g] = goh[yh]

    def scores(t):
        return nt(q2[...], kv[t, 0]) * SCALE

    def row_first():
        sc = scores(0)
        ok = iota((256, TOK), 0) % TOK >= iota((256, TOK), 1)
        sc = jnp.where(ok, sc, NEG)
        mx = jnp.max(sc, axis=1, keepdims=True)
        p = jnp.exp(sc - mx)
        m_ref[...] = mx
        l_ref[...] = jnp.sum(p, axis=1, keepdims=True)
        acc2[...] = nn(p.astype(BF16), kv[0, 1])

    def row_step(t):
        @pl.when(cg >= t)
        def _():
            for i in range(2):
                copy(kv.at[t, i], kv.at[t, i], row_s.at[t, i], row_r.at[t, i], (s - 1, m)).wait_recv()

                @pl.when(cg < 7)
                def _():
                    row_copy(t, i).start()

            sc = scores(t)
            old = m_ref[...]
            mx = jnp.maximum(old, jnp.max(sc, axis=1, keepdims=True))
            p = jnp.exp(sc - mx)
            w = jnp.exp(old - mx)
            m_ref[...] = mx
            l_ref[...] = l_ref[...] * w + jnp.sum(p, axis=1, keepdims=True)
            acc2[...] = acc2[...] * w + nn(p.astype(BF16), kv[t, 1])

    row_first()

    def finish_dattn():
        d = part[m].astype(F32)
        for i in range(1, 4):
            o = (m + i) % 4
            copy(part.at[o], mpin.at[o], mp_s.at[o], mp_r.at[o], (s, o)).wait_recv()
            d = d + mpin[o].astype(F32)
        d = d.astype(BF16).astype(F32)
        dat[...] = d
        d2[...] = head_pair(d)
        cold[...] = d.reshape(16, 8, WP)
        each(16, lambda i: col_send(cold, coldin, cd_s, cd_r, i).start())
        coldin[r] = cold[r]

    finish_dattn()
    lax.fori_loop(1, 5, lambda t, c: (row_step(t), c)[1], 0)

    def col_part(i):
        c = colin[...].astype(F32)
        return c[:, 8 * i : 8 * i + 8, :].reshape(TOK, WP)

    def col_forward():
        each(16, lambda i: col_wait(colx, colin, ca_s, ca_r, i))
        cq2 = head_pair(col_part(0))
        ck = col_part(1).astype(BF16)
        cv = col_part(2).astype(BF16)
        sc = nt(cq2, ck) * SCALE
        qi = iota((256, TOK), 0) % TOK
        ki = iota((256, TOK), 1)
        ok = (qi % 8 == ki % 8) & (ki // 8 < qi // 8)
        mx = jnp.max(jnp.where(ok, sc, NEG), axis=1, keepdims=True)
        p = jnp.where(ok, jnp.exp(sc - mx), 0.0)
        tot = jnp.sum(p, axis=1, keepdims=True)
        some = tot > 0.0
        safe = jnp.where(some, tot, 1.0)
        o = pick(nn(p.astype(BF16), cv) / safe)
        lse = jnp.where(some, mx + jnp.log(safe), NEG)
        lane = iota((TOK, WP), 1)
        o = jnp.where(lane < W, o, jnp.where(lane < 340, lse[:TOK], lse[TOK:]))
        colo[...] = o.reshape(16, 8, WP)
        each(16, lambda i: col_send(colo, coloin, co_s, co_r, i).start())
        coloin[r] = colo[r]

    col_forward()
    lax.fori_loop(5, 8, lambda t, c: (row_step(t), c)[1], 0)

    def ag_copy(i):
        o = (m + i) % 4
        return copy(att.at[m], att.at[m], ag_s.at[o], ag_r.at[m], (s, o))

    def merge():
        each(16, lambda i: col_wait(colo, coloin, co_s, co_r, i))
        far = coloin[...].reshape(TOK, WP)
        lane = iota((TOK, WP), 1)
        d = dat[...]
        near = pick(acc2[...])
        lses, near_w, far_w = [], [], []
        for h in range(2):
            lo = W + 40 * h
            here = (lane >= lo) & (lane < lo + 40)
            fl = jnp.max(jnp.where(here, far, -3e38), axis=1, keepdims=True)
            mr = m_ref[h * TOK : h * TOK + TOK, :]
            nl = mr + jnp.log(l_ref[h * TOK : h * TOK + TOK, :])
            top = jnp.maximum(nl, fl)
            lse = top + jnp.log(jnp.exp(nl - top) + jnp.exp(fl - top))
            lses.append(lse)
            near_w.append(jnp.exp(mr - lse))
            far_w.append(jnp.exp(fl - lse))
        nw = jnp.where(lane < HD, near_w[0], near_w[1])
        fw = jnp.where(lane < HD, far_w[0], far_w[1])
        a = jnp.where(lane < W, near * nw + far * fw, 0.0).astype(BF16)
        att[m] = a
        each(4, lambda i: ag_copy(i).start())
        prod = a.astype(F32) * d
        d0 = jnp.sum(jnp.where(lane < HD, prod, 0.0), axis=1, keepdims=True)
        d1 = jnp.sum(jnp.where((lane >= HD) & (lane < W), prod, 0.0), axis=1, keepdims=True)
        ln = iota((TOK, TOK), 1)
        info = jnp.where(ln < 64, jnp.where(ln < 32, lses[0], lses[1]), jnp.where(ln < 96, d0, d1))
        coli[...] = info.reshape(16, 8, TOK)
        each(16, lambda i: col_send(coli, coliin, ci_s, ci_r, i).start())
        coliin[r] = coli[r]
        info_t[...] = info.T
        gq2[...] = jnp.zeros_like(gq2)

    merge()

    def stats(it):
        lse = jnp.concatenate([it[0:1], it[32:33]], axis=1)
        delta = jnp.concatenate([it[64:65], it[96:97]], axis=1)
        return lse, delta

    def row_own(u):
        @pl.when(cg >= u)
        def _():
            t = cg - u
            lse, delta = stats(info_t[...])
            k_t, v_t = kv[t, 0], kv[t, 1]
            sc = nt(k_t, q2[...]) * SCALE
            ok = (t > 0) | (iota((TOK, 256), 0) <= iota((TOK, 256), 1) % TOK)
            p = jnp.where(ok, jnp.exp(sc - lse), 0.0)
            dp = nt(v_t, d2[...])
            ds = (p * (dp - delta)).astype(BF16)
            own[u, 0] = nn(ds, q2[...]) * SCALE
            own[u, 1] = nn(p.astype(BF16), d2[...])
            gq2[...] += tn(ds, k_t)

    def rb_copy(u, i):
        return copy(rbs.at[u, i], rbin.at[u, i], rb_s.at[u, i], rb_r.at[u, i], (s - 1, m))

    def row_chain(u):
        @pl.when(cg >= u)
        def _():
            for i in range(2):
                @pl.when(cg < 7)
                def _():
                    rb_copy(u, i).wait_recv()
                    own[u, i] += rbin[u, i].astype(F32)

                @pl.when(cg > u)
                def _():
                    rbs[u, i] = own[u, i].astype(BF16)
                    rb_copy(u, i).start()

    def gw_copy(i):
        o = (g + i) % 8
        return copy(att.at[o % 4], gwin.at[g], gw_s.at[o], gw_r.at[g], g_dev(o))

    def gather_attn():
        for i in range(1, 4):
            o = (m + i) % 4
            copy(att.at[o], att.at[o], ag_s.at[o], ag_r.at[o], (s, o)).wait_recv()
        each(8, lambda i: gw_copy(i).start())
        gwin[g] = att[x]

    def layer():
        full = jnp.concatenate([att[i].astype(F32)[:, :W] for i in range(4)], axis=1).astype(BF16)
        lay_ref[...] = nt(full, w_ref[...]).astype(BF16)

    def z1_copy(i):
        o = (zr + i) % 4
        return copy(gz1.at[o], z1in.at[zr], z1_s.at[o], z1_r.at[zr], z_dev(zq * 4 + o))

    def gw_product():
        def arrived(i):
            o = (g + i) % 8
            copy(goh.at[0], goin.at[o], go_s.at[o], go_r.at[o], g_dev(o)).wait_recv()
            copy(att.at[0], gwin.at[o], gw_s.at[o], gw_r.at[o], g_dev(o)).wait_recv()

        each(8, arrived)
        prod = tn(goin[...].reshape(8 * TOK, WP), gwin[...].reshape(8 * TOK, WP)).astype(BF16)
        to = iota((512, WP), 0)
        i5 = to % 8
        xx = (to // 8) % 4
        qq = (to // 32) % 4
        rr = to // 128
        src = jnp.where(i5 < 5, (xx * 16 + qq * 4 + rr) * 5 + i5, -1)
        perm = (src == iota((512, WP), 1)).astype(F32).astype(BF16)
        gz1[...] = nn(perm, prod).astype(BF16).reshape(4, TOK, WP)
        each(4, lambda i: z1_copy(i).start())

    def z2_copy(i):
        o = (zq + i) % 4
        return copy(gz2.at[o], z2in.at[zq], z2_s.at[o], z2_r.at[zq], z_dev(o * 4 + zr))

    def gw_level1():
        t = gz1[zr].astype(F32)
        for i in range(1, 4):
            o = (zr + i) % 4
            copy(gz1.at[o], z1in.at[o], z1_s.at[o], z1_r.at[o], z_dev(zq * 4 + o)).wait_recv()
            t = t + z1in[o].astype(F32)
        gz2[...] = t.astype(BF16).reshape(4, 32, WP)
        each(4, lambda i: z2_copy(i).start())

    def fx_copy(i):
        o = (x + i) % 4
        return copy(gfx.at[o], fxin.at[x], fx_s.at[o], fx_r.at[x], x_dev(o))

    def gw_level2():
        t = gz2[zq].astype(F32)
        for i in range(1, 4):
            o = (zq + i) % 4
            copy(gz2.at[o], z2in.at[o], z2_s.at[o], z2_r.at[o], z_dev(o * 4 + zr)).wait_recv()
            t = t + z2in[o].astype(F32)
        gfx[...] = t.reshape(4, 8, WP)
        each(4, lambda i: fx_copy(i).start())
        fxin[x] = gfx[x]

    def gw_finish():
        for i in range(1, 4):
            o = (x + i) % 4
            copy(gfx.at[o], fxin.at[o], fx_s.at[o], fx_r.at[o], x_dev(o)).wait_recv()
        gw_ref[...] = jnp.concatenate([fxin[i][:, :W] for i in range(4)], axis=1)[:5]

    def col_backward():
        each(16, lambda i: col_wait(cold, coldin, cd_s, cd_r, i))
        each(16, lambda i: col_wait(coli, coliin, ci_s, ci_r, i))
        cq2 = head_pair(col_part(0))
        ck = col_part(1).astype(BF16)
        cv = col_part(2).astype(BF16)
        cd2 = head_pair(coldin[...].reshape(TOK, WP))
        lse, delta = stats(coliin[...].reshape(TOK, TOK).T)
        sc = nt(ck, cq2) * SCALE
        ki = iota((TOK, 256), 0)
        qi = iota((TOK, 256), 1) % TOK
        ok = (qi % 8 == ki % 8) & (ki // 8 < qi // 8)
        p = jnp.where(ok, jnp.exp(sc - lse), 0.0)
        dp = nt(cv, cd2)
        ds = (p * (dp - delta)).astype(BF16)
        ggk = nn(ds, cq2) * SCALE
        ggv = nn(p.astype(BF16), cd2)
        ggq = pick(tn(ds, ck)) * SCALE
        out = [t.reshape(16, 8, WP) for t in (ggq, ggk, ggv, jnp.zeros_like(ggq))]
        colg[...] = jnp.concatenate(out, axis=1).astype(BF16)
        each(16, lambda i: col_send(colg, colgin, cg_s, cg_r, i).start())
        colgin[r] = colg[r]

    row_own(0)

    @pl.when(cg == 7)
    def _():
        row_chain(0)

    gather_attn()

    @pl.when(cg < 4)
    def _():
        col_backward()
        gw_product()

    layer()

    @pl.when(cg < 7)
    def _():
        row_chain(0)

    def both(u):
        row_own(u)
        row_chain(u)

    lax.fori_loop(1, 3, lambda u, c: (both(u), c)[1], 0)

    @pl.when(cg >= 4)
    def _():
        col_backward()
        gw_product()

    lax.fori_loop(3, 8, lambda u, c: (both(u), c)[1], 0)
    gw_level1()
    gw_level2()

    each(16, lambda i: col_wait(colg, colgin, cg_s, cg_r, i))
    home = colgin[...].astype(F32)
    hq, hk, hv = (home[:, 8 * i : 8 * i + 8, :].reshape(TOK, WP) for i in range(3))
    gq_ref[...] = (pick(gq2[...]) * SCALE + hq)[:, :W].astype(BF16)
    gk_ref[...] = (own[cg, 0] + hk)[:, :W].astype(BF16)
    gv_ref[...] = (own[cg, 1] + hv)[:, :W].astype(BF16)
    gw_finish()

    def sent(t, c):
        @pl.when((cg < 7) & (t <= cg))
        def _():
            row_copy(t, 0).wait_send()
            row_copy(t, 1).wait_send()

        @pl.when(t < cg)
        def _():
            rb_copy(t, 0).wait_send()
            rb_copy(t, 1).wait_send()

        return c

    lax.fori_loop(0, 8, sent, 0)
    for f in (mp_copy, ag_copy, z1_copy, z2_copy, fx_copy):
        each(4, lambda i, f=f: f(i).wait_send())
    for f in (go_copy, gw_copy):
        each(8, lambda i, f=f: f(i).wait_send())

    def col_sent(i):
        col_send(colx, colin, ca_s, ca_r, i).wait_send()
        col_send(cold, coldin, cd_s, cd_r, i).wait_send()
        col_send(colo, coloin, co_s, co_r, i).wait_send()
        col_send(coli, coliin, ci_s, ci_r, i).wait_send()
        col_send(colg, colgin, cg_s, cg_r, i).wait_send()

    each(16, col_sent)


def body(queries, keys, values, weight_out, grad_out):
    vm = pl.BlockSpec(memory_space=pltpu.VMEM)
    dma = pltpu.SemaphoreType.DMA
    vmem = pltpu.VMEM
    out = jax.ShapeDtypeStruct
    scratch = [
        vmem((8, 2, TOK, WP), BF16),
        vmem((256, WP), BF16),
        vmem((256, WP), BF16),
        vmem((256, WP), F32),
        vmem((256, 1), F32),
        vmem((256, 1), F32),
        vmem((256, WP), F32),
        vmem((8, 2, TOK, WP), F32),
        vmem((4, TOK, WP), BF16),
        vmem((4, TOK, WP), BF16),
        vmem((16, 32, WP), BF16),
        vmem((16, 32, WP), BF16),
        vmem((16, 8, WP), F32),
        vmem((16, 8, WP), F32),
        vmem((16, 8, WP), F32),
        vmem((16, 8, WP), F32),
        vmem((16, 8, TOK), F32),
        vmem((16, 8, TOK), F32),
        vmem((16, 32, WP), BF16),
        vmem((16, 32, WP), BF16),
        vmem((4, TOK, WP), BF16),
        vmem((2, TOK, WP), BF16),
        vmem((8, TOK, WP), BF16),
        vmem((8, TOK, WP), BF16),
        vmem((4, TOK, WP), BF16),
        vmem((4, TOK, WP), BF16),
        vmem((4, 32, WP), BF16),
        vmem((4, 32, WP), BF16),
        vmem((4, 8, WP), F32),
        vmem((4, 8, WP), F32),
        vmem((8, 2, TOK, WP), BF16),
        vmem((8, 2, TOK, WP), BF16),
        vmem((TOK, TOK), F32),
        vmem((TOK, WP), F32),
    ]
    sems = [dma((8, 2))] * 4 + [dma((4,))] * 4 + [dma((16,))] * 10 + [dma((8,))] * 4 + [dma((4,))] * 6
    return pl.pallas_call(
        kernel,
        out_shape=(
            out((TOK, 640), BF16),
            out((TOK, W), BF16),
            out((TOK, W), BF16),
            out((TOK, W), BF16),
            out((5, 4 * W), F32),
        ),
        in_specs=[vm] * 5,
        out_specs=[vm] * 5,
        scratch_shapes=scratch + sems,
        compiler_params=pltpu.CompilerParams(
            collective_id=0, has_side_effects=True, vmem_limit_bytes=50 * 2**20
        ),
    )(queries, keys, values, weight_out, grad_out)


def solution(mesh):
    placed = (P("seq", "mp"), P("seq", "mp"), P("seq", "mp"), P("mp", None), P("seq", "mp"))
    return jax.shard_map(
        body,
        mesh=mesh,
        in_specs=placed,
        out_specs=(
            P("seq", "mp"),
            P("seq", "mp"),
            P("seq", "mp"),
            P("seq", "mp"),
            P(("mp", "seq"), None),
        ),
        check_vma=False,
    )
```

```python
import jax
import jax.numpy as jnp
from jax import lax
from jax.experimental import pallas as pl
from jax.experimental.pallas import tpu as pltpu
from jax.sharding import PartitionSpec as P

MESH = pl.DeviceIdType.MESH
HD = 150
W = 300
WP = 384
WR = 304
TOK = 128
NEG = -1e30
SCALE = HD ** (-0.5)
F32 = jnp.float32
BF16 = jnp.bfloat16


def nn(a, b):
    return jnp.dot(a, b, preferred_element_type=F32)


def nt(a, b):
    return lax.dot_general(a, b, (((1,), (1,)), ((), ())), preferred_element_type=F32)


def tn(a, b):
    return lax.dot_general(a, b, (((0,), (0,)), ((), ())), preferred_element_type=F32)


def iota(shape, dim):
    return lax.broadcasted_iota(jnp.int32, shape, dim)


def head_pair(x):
    lane = iota(x.shape, 1)
    a = jnp.where(lane < HD, x, 0.0)
    b = jnp.where((lane >= HD) & (lane < W), x, 0.0)
    return jnp.concatenate([a, b], axis=0).astype(BF16)


def head_columns(x):
    row = iota(x.shape, 0)
    a = jnp.where(row < HD, x, 0.0)
    b = jnp.where((row >= HD) & (row < W), x, 0.0)
    return jnp.concatenate([a, b], axis=1).astype(BF16)


def pick(x2):
    n = x2.shape[0] // 2
    lane = iota((n, WP), 1)
    return jnp.where(lane < HD, x2[:n], x2[n:])


def each(n, f):
    lax.fori_loop(1, n, lambda i, c: (f(i), c)[1], 0)


class Exchange:
    def __init__(self, n, out, into):
        self.n, self.out, self.into = n, out, into

    def start(self):
        each(self.n, lambda i: self.out(i).start())

    def arrive(self):
        each(self.n, lambda i: self.into(i).wait_recv())

    def sent(self):
        each(self.n, lambda i: self.out(i).wait_send())


def kernel(
    q_hbm, k_hbm, v_hbm, w_hbm, go_hbm,
    lay_ref, gq_ref, gk_ref, gv_ref, gw_ref,
    xin, w_ref, go_ref, kv, q2, q2t, d2, d2t, acc2, m_ref, l_ref, gq2, own,
    part, mpin, cola, colain, colxin, cold, coldin, colo, coloin, coli, coliin,
    colg, colgin, colh, colhin, viax, viah,
    att, goh, goin, gwin, gz1, z1in, gz2, z2in, gfx, fxin, rbs, rbin, info, dat,
    in_s, row_s, row_r, rb_s, rb_r, mp_s, mp_r, ag_s, ag_r,
    ca_s, ca_r, cx_s, cx_r, cd_s, cd_r, co_s, co_r, ci_s, ci_r, cg_s, cg_r, ch_s, ch_r, hop_s, hop_r, vx_s, vh_s,
    go_s, go_r, gw_s, gw_r, z1_s, z1_r, z2_s, z2_r, fx_s, fx_r,
):
    s = lax.axis_index("seq")
    m = lax.axis_index("mp")
    cg = s % 8
    yh, x, z = s // 64, (s // 16) % 4, s % 16
    zq, zr = z // 4, z % 4
    g = yh * 4 + x

    def copy(src, dst, ss, rs, dev):
        return pltpu.make_async_remote_copy(
            src_ref=src, dst_ref=dst, send_sem=ss, recv_sem=rs, device_id=dev, device_id_type=MESH
        )

    def exchange(n, me, dev, src, dst, ss, rs):
        def other(i):
            return (me + i) % n

        def out(i):
            o = other(i)
            return copy(src(o), dst.at[me], ss.at[o], rs.at[me], dev(o))

        def into(i):
            o = other(i)
            return copy(src(o), dst.at[o], ss.at[o], rs.at[o], dev(o))

        return Exchange(n, out, into)

    def g_dev(o):
        return ((o // 4) * 64 + (o % 4) * 16 + z, m)

    def z_dev(o):
        return (yh * 64 + x * 16 + o, m)

    def mp_dev(o):
        return (s, o)

    def columns(src, dst, ss, rs):
        return exchange(8, g, g_dev, lambda o: src.at[o], dst, ss, rs)

    def far_dev(o, d):
        return ((o // 4) * 64 + (o % 4) * 16 + (z + 16 + d) % 16, m)

    class Across:
        def __init__(self, src, dst, via, d, ss, rs, vs, k):
            self.src, self.dst, self.via, self.d, self.ss, self.rs, self.vs, self.k = src, dst, via, d, ss, rs, vs, k

        def hop(self):
            return copy(self.src(pl.ds(4, 4)), self.via, hop_s.at[self.k], hop_r.at[self.k], far_dev(g, self.d))

        def straight(self, o):
            return copy(self.src(o), self.dst.at[g], self.ss.at[o], self.rs.at[g], far_dev(o, 8))

        def onward(self, o):
            return copy(self.via.at[o], self.dst.at[g], self.vs.at[o], self.rs.at[g], far_dev(o + 4, 7 * self.d))

        def start(self):
            self.hop().start()
            lax.fori_loop(0, 4, lambda o, c: (self.straight(o).start(), c)[1], 0)

        def relay(self):
            self.hop().wait_recv()
            lax.fori_loop(0, 4, lambda o, c: (self.onward(o).start(), c)[1], 0)

        def arrive(self):
            def one(o, c):
                copy(self.src(o), self.dst.at[o], self.ss.at[o], self.rs.at[o], far_dev(o, 8)).wait_recv()
                return c

            lax.fori_loop(0, 8, one, 0)

        def sent(self):
            def one(o, c):
                self.straight(o).wait_send()
                self.onward(o).wait_send()
                return c

            self.hop().wait_send()
            lax.fori_loop(0, 4, one, 0)

    ex_mp = exchange(4, m, mp_dev, lambda o: part.at[o], mpin, mp_s, mp_r)
    ex_ag = exchange(4, m, mp_dev, lambda o: att.at[m], att, ag_s, ag_r)
    ex_ca = columns(cola, colain, ca_s, ca_r)
    ex_cx = Across(lambda o: cola.at[o, pl.ds(16, 32)], colxin, viax, -1, cx_s, cx_r, vx_s, 0)
    ex_cd = columns(cold, coldin, cd_s, cd_r)
    ex_co = columns(colo, coloin, co_s, co_r)
    ex_ci = columns(coli, coliin, ci_s, ci_r)
    ex_cg = columns(colg, colgin, cg_s, cg_r)
    ex_ch = Across(lambda o: colh.at[o], colhin, viah, 1, ch_s, ch_r, vh_s, 1)
    ex_go = exchange(8, g, g_dev, lambda o: goh.at[o // 4], goin, go_s, go_r)
    ex_gw = exchange(8, g, g_dev, lambda o: att.at[o % 4], gwin, gw_s, gw_r)
    ex_z1 = exchange(4, zr, lambda o: z_dev(zq * 4 + o), lambda o: gz1.at[o], z1in, z1_s, z1_r)
    ex_z2 = exchange(4, zq, lambda o: z_dev(o * 4 + zr), lambda o: gz2.at[o], z2in, z2_s, z2_r)
    ex_fx = exchange(4, x, lambda o: (yh * 64 + o * 16 + z, m), lambda o: gfx.at[o], fxin, fx_s, fx_r)

    loads = [
        pltpu.make_async_copy(a, b, in_s.at[i])
        for i, (a, b) in enumerate(
            (
                (q_hbm, xin.at[0]), (k_hbm, xin.at[1]), (v_hbm, xin.at[2]),
                (go_hbm, go_ref), (w_hbm, w_ref),
            )
        )
    ]
    for c in loads:
        c.start()
    kv[:, :, 288:, :] = jnp.zeros((8, 2, WP - 288, TOK), BF16)
    bar = pltpu.get_barrier_semaphore()

    def greet(dev):
        pl.semaphore_signal(bar, inc=1, device_id=dev, device_id_type=MESH)

    each(8, lambda i: greet(g_dev((g + i) % 8)))

    def greet_sender(o, c):
        @pl.when(g < 4)
        def _():
            greet(far_dev(o, 8))

        @pl.when(g >= 4)
        def _():
            greet(far_dev(o, 7))
            greet(far_dev(o, -7))

        return c

    lax.fori_loop(0, 8, greet_sender, 0)
    greet(far_dev(g, 1))
    greet(far_dev(g, -1))
    each(4, lambda i: greet((s, (m + i) % 4)))
    each(4, lambda i: greet(z_dev(zq * 4 + (zr + i) % 4)))
    each(4, lambda i: greet(z_dev(((zq + i) % 4) * 4 + zr)))

    @pl.when(cg > 0)
    def _():
        greet((s - 1, m))

    @pl.when(cg < 7)
    def _():
        greet((s + 1, m))

    for c in loads[:3]:
        c.wait()
    kv[0, 0, :W, :] = xin[1]
    kv[0, 1, :W, :] = xin[2]
    fill = jnp.zeros((WP - W, TOK), F32)
    qt = jnp.concatenate([xin[0].astype(F32), fill], axis=0)
    q2t[...] = head_columns(qt)
    q32 = qt.T
    k32 = kv[0, 0].astype(F32).T
    v32 = kv[0, 1].astype(F32).T
    q2[...] = head_pair(q32)
    for i, t in enumerate((q32, k32, v32)):
        cola[:, 16 * i : 16 * i + 16, :] = t.astype(BF16).reshape(8, 16, WP)
    for c in loads[3:]:
        c.wait()
    pg = nt(go_ref[...], w_ref[...])
    lanes = jnp.zeros((TOK, WP - W), F32)
    for i in range(4):
        part[i] = jnp.concatenate([pg[:, W * i : W * i + W], lanes], axis=1).astype(BF16)
    go_t = go_ref[...].astype(F32).T.astype(BF16)
    goh[0] = go_t[:320]
    goh[1] = go_t[320:]

    links = (cg > 0).astype(jnp.int32) + (cg < 7).astype(jnp.int32)
    pl.semaphore_wait(bar, 7 + 4 + 8 + 2 + 3 + 3 + 3 + links)

    def row_copy(t, i):
        return copy(
            kv.at[t, i, pl.ds(0, WR)], kv.at[t + 1, i, pl.ds(0, WR)],
            row_s.at[t, i], row_r.at[t + 1, i], (s + 1, m),
        )

    def row_arrival(t, i):
        return copy(
            kv.at[t, i, pl.ds(0, WR)], kv.at[t, i, pl.ds(0, WR)],
            row_s.at[t, i], row_r.at[t, i], (s - 1, m),
        )

    @pl.when(cg < 7)
    def _():
        row_copy(0, 0).start()
        row_copy(0, 1).start()

    ex_cx.start()
    ex_mp.start()
    ex_ca.start()
    colain[g] = cola[g]
    ex_go.start()
    goin[g] = goh[yh]

    def scores(t):
        return nn(q2[...], kv[t, 0]) * SCALE

    def row_first():
        sc = scores(0)
        ok = iota((256, TOK), 0) % TOK >= iota((256, TOK), 1)
        sc = jnp.where(ok, sc, NEG)
        mx = jnp.max(sc, axis=1, keepdims=True)
        p = jnp.exp(sc - mx)
        m_ref[...] = mx
        l_ref[...] = jnp.sum(p, axis=1, keepdims=True)
        acc2[...] = nt(p.astype(BF16), kv[0, 1])

    def row_step(t):
        @pl.when(cg >= t)
        def _():
            for i in range(2):
                row_arrival(t, i).wait_recv()

                @pl.when(cg < 7)
                def _():
                    row_copy(t, i).start()

            sc = scores(t)
            old = m_ref[...]
            mx = jnp.maximum(old, jnp.max(sc, axis=1, keepdims=True))
            p = jnp.exp(sc - mx)
            w = jnp.exp(old - mx)
            m_ref[...] = mx
            l_ref[...] = l_ref[...] * w + jnp.sum(p, axis=1, keepdims=True)
            acc2[...] = acc2[...] * w + nt(p.astype(BF16), kv[t, 1])

    def row_steps(lo, hi):
        lax.fori_loop(lo, hi, lambda t, c: (row_step(t), c)[1], 0)

    def finish_dattn():
        ex_mp.arrive()
        d = part[m].astype(F32)
        for i in range(1, 4):
            d = d + mpin[(m + i) % 4].astype(F32)
        d = d.astype(BF16).astype(F32)
        dat[...] = d
        d2[...] = head_pair(d)
        d2t[...] = head_columns(d.T)
        cold[...] = d.astype(BF16).reshape(8, 16, WP)
        ex_cd.start()
        coldin[g] = cold[g]

    def column_rows(ref, i):
        return ref[:, 16 * i : 16 * i + 16, :].reshape(TOK, WP)

    def column_operands():
        ck = jnp.concatenate([column_rows(colain, 1), column_rows(colxin, 0)], axis=0)
        cv = jnp.concatenate([column_rows(colain, 2), column_rows(colxin, 1)], axis=0)
        return head_pair(column_rows(colain, 0).astype(F32)), ck, cv

    def column_mask(shape, qdim):
        qi = iota(shape, qdim) % TOK
        kj = iota(shape, 1 - qdim)
        ki = kj % TOK
        later = jnp.where(kj < TOK, 0, z // 8)
        return (qi % 16 == ki % 16) & (ki // 16 < qi // 16 + later)

    def col_forward():
        ex_ca.arrive()
        ex_cx.arrive()
        cq2, ck, cv = column_operands()
        sc = nt(cq2, ck) * SCALE
        ok = column_mask((256, 256), 0)
        mx = jnp.max(jnp.where(ok, sc, NEG), axis=1, keepdims=True)
        p = jnp.where(ok, jnp.exp(sc - mx), 0.0)
        tot = jnp.sum(p, axis=1, keepdims=True)
        some = tot > 0.0
        safe = jnp.where(some, tot, 1.0)
        o = pick(nn(p.astype(BF16), cv) / safe)
        lse = jnp.where(some, mx + jnp.log(safe), NEG)
        lane = iota((TOK, WP), 1)
        o = jnp.where(lane < W, o, jnp.where(lane < 340, lse[:TOK], lse[TOK:]))
        colo[...] = o.reshape(8, 16, WP)
        ex_co.start()
        coloin[g] = colo[g]

    def merge():
        ex_co.arrive()
        far = coloin[...].reshape(TOK, WP)
        lane = iota((TOK, WP), 1)
        d = dat[...]
        near = pick(acc2[...])
        lses, near_w, far_w = [], [], []
        for h in range(2):
            lo = W + 40 * h
            here = (lane >= lo) & (lane < lo + 40)
            fl = jnp.max(jnp.where(here, far, -3e38), axis=1, keepdims=True)
            mr = m_ref[h * TOK : h * TOK + TOK, :]
            nl = mr + jnp.log(l_ref[h * TOK : h * TOK + TOK, :])
            top = jnp.maximum(nl, fl)
            lse = top + jnp.log(jnp.exp(nl - top) + jnp.exp(fl - top))
            lses.append(lse)
            near_w.append(jnp.exp(mr - lse))
            far_w.append(jnp.exp(fl - lse))
        nw = jnp.where(lane < HD, near_w[0], near_w[1])
        fw = jnp.where(lane < HD, far_w[0], far_w[1])
        a = jnp.where(lane < W, near * nw + far * fw, 0.0).astype(BF16)
        att[m] = a
        ex_ag.start()
        prod = a.astype(F32) * d
        d0 = jnp.sum(jnp.where(lane < HD, prod, 0.0), axis=1, keepdims=True)
        d1 = jnp.sum(jnp.where((lane >= HD) & (lane < W), prod, 0.0), axis=1, keepdims=True)
        ln = iota((TOK, TOK), 1)
        both = jnp.where(ln < 64, jnp.where(ln < 32, lses[0], lses[1]), jnp.where(ln < 96, d0, d1))
        coli[...] = both.reshape(8, 16, TOK)
        ex_ci.start()
        coliin[g] = coli[g]
        info[...] = both
        gq2[...] = jnp.zeros_like(gq2)

    def stats(a):
        pair = [jnp.concatenate([a[:, i : i + 1], a[:, i + 32 : i + 33]], axis=0) for i in (0, 64)]
        return pair[0], pair[1]

    def row_own(u):
        @pl.when(cg >= u)
        def _():
            t = cg - u
            lse, delta = stats(info[...])
            k_t, v_t = kv[t, 0], kv[t, 1]
            ok = (t > 0) | (iota((256, TOK), 0) % TOK >= iota((256, TOK), 1))
            p = jnp.where(ok, jnp.exp(scores(t) - lse), 0.0)
            dp = nn(d2[...], v_t)
            ds = (p * (dp - delta)).astype(BF16)
            own[u, 0] = (nn(q2t[...], ds) * SCALE)[:WR]
            own[u, 1] = nn(d2t[...], p.astype(BF16))[:WR]
            gq2[...] += nt(ds, k_t)

    def rb_copy(u, i):
        return copy(rbs.at[u, i], rbin.at[u, i], rb_s.at[u, i], rb_r.at[u, i], (s - 1, m))

    def row_chain(u):
        @pl.when(cg >= u)
        def _():
            for i in range(2):
                @pl.when(cg < 7)
                def _():
                    rb_copy(u, i).wait_recv()
                    own[u, i] += rbin[u, i].astype(F32)

                @pl.when(cg > u)
                def _():
                    rbs[u, i] = own[u, i].astype(BF16)
                    rb_copy(u, i).start()

    def gather_attn():
        ex_ag.arrive()
        ex_gw.start()
        gwin[g] = att[x]

    def layer():
        full = jnp.concatenate([att[i].astype(F32)[:, :W] for i in range(4)], axis=1).astype(BF16)
        lay_ref[...] = nn(full, w_ref[...]).astype(BF16)

    def gw_product():
        ex_go.arrive()
        ex_gw.arrive()
        prod = nn(goin[0], gwin[0])
        for i in range(1, 8):
            prod = prod + nn(goin[i], gwin[i])
        to = iota((320, 320), 0)
        src = ((to // 5 % 4) * 16 + (to // 20 % 4) * 4 + to // 80) * 5 + to % 5
        perm = (src == iota((320, 320), 1)).astype(F32).astype(BF16)
        gz1[...] = nn(perm, prod.astype(BF16)).astype(BF16).reshape(4, 80, WP)
        ex_z1.start()

    def gw_level1():
        ex_z1.arrive()
        t = gz1[zr].astype(F32)
        for i in range(1, 4):
            t = t + z1in[(zr + i) % 4].astype(F32)
        to = iota((TOK, 80), 0)
        src = jnp.where(to % 8 < 5, to // 8 * 5 + to % 8, -1)
        perm = (src == iota((TOK, 80), 1)).astype(F32).astype(BF16)
        gz2[...] = nn(perm, t.astype(BF16)).astype(BF16).reshape(4, 32, WP)
        ex_z2.start()

    def gw_level2():
        ex_z2.arrive()
        t = gz2[zq].astype(F32)
        for i in range(1, 4):
            t = t + z2in[(zq + i) % 4].astype(F32)
        gfx[...] = t.reshape(4, 8, WP)
        ex_fx.start()
        fxin[x] = gfx[x]

    def gw_finish():
        ex_fx.arrive()
        gw_ref[...] = jnp.concatenate([fxin[i][:, :W] for i in range(4)], axis=1)[:5]

    def col_backward():
        ex_ci.arrive()
        ex_cd.arrive()
        cq2, ck, cv = column_operands()
        cd2 = head_pair(coldin[...].reshape(TOK, WP).astype(F32))
        both = coliin[...].reshape(TOK, TOK).T
        lse = jnp.concatenate([both[0:1], both[32:33]], axis=1)
        delta = jnp.concatenate([both[64:65], both[96:97]], axis=1)
        sc = nt(ck, cq2) * SCALE
        ok = column_mask((256, 256), 1)
        p = jnp.where(ok, jnp.exp(sc - lse), 0.0)
        dp = nt(cv, cd2)
        ds = (p * (dp - delta)).astype(BF16)
        ggk = nn(ds, cq2) * SCALE
        ggv = nn(p.astype(BF16), cd2)
        ggq = pick(tn(ds, ck)) * SCALE
        for i, t in enumerate((ggk, ggv)):
            colh[:, 16 * i : 16 * i + 16, :] = t[TOK:].astype(BF16).reshape(8, 16, WP)
        ex_ch.start()
        for i, t in enumerate((ggq, ggk[:TOK], ggv[:TOK])):
            colg[:, 16 * i : 16 * i + 16, :] = t.astype(BF16).reshape(8, 16, WP)
        ex_cg.start()
        colgin[g] = colg[g]

    def both(u):
        row_own(u)
        row_chain(u)

    def results():
        ex_cg.arrive()
        ex_ch.arrive()
        hq, hk, hv = (column_rows(colgin, i).astype(F32) for i in range(3))
        hk = hk + column_rows(colhin, 0).astype(F32)
        hv = hv + column_rows(colhin, 1).astype(F32)
        gq_ref[...] = (pick(gq2[...]) * SCALE + hq).T[:W].astype(BF16)
        gk_ref[...] = (own[cg, 0] + hk.T[:WR])[:W].astype(BF16)
        gv_ref[...] = (own[cg, 1] + hv.T[:WR])[:W].astype(BF16)

    def tick(u):
        row_own(u)

        @pl.when(u + cg >= 7)
        def _():
            row_chain(u + cg - 7)

    def ticks(lo, hi):
        lax.fori_loop(lo, hi, lambda u, c: (tick(u), c)[1], 0)

    row_first()
    ex_cx.relay()
    finish_dattn()
    row_steps(1, 3)
    col_forward()
    row_steps(3, 8)
    merge()
    gather_attn()
    ticks(0, 1)
    col_backward()
    ticks(1, 2)
    ex_ch.relay()
    gw_product()
    ticks(2, 5)
    gw_level1()
    ticks(5, 7)
    gw_level2()
    ticks(7, 8)
    layer()
    results()
    gw_finish()

    def sent(t, c):
        @pl.when((cg < 7) & (t <= cg))
        def _():
            row_copy(t, 0).wait_send()
            row_copy(t, 1).wait_send()

        @pl.when(t < cg)
        def _():
            rb_copy(t, 0).wait_send()
            rb_copy(t, 1).wait_send()

        return c

    lax.fori_loop(0, 8, sent, 0)
    for e in (ex_mp, ex_ag, ex_ca, ex_cx, ex_cd, ex_co, ex_ci, ex_cg, ex_ch, ex_go, ex_gw, ex_z1, ex_z2, ex_fx):
        e.sent()


def hand_over(*refs):
    for a, b in zip(refs[:5], refs[5:]):
        b[...] = a[...]


def body(queries, keys, values, weight_out, grad_out):
    vm = pl.BlockSpec(memory_space=pltpu.VMEM)
    hbm = pl.BlockSpec(memory_space=pltpu.HBM)
    dma = pltpu.SemaphoreType.DMA
    vmem = pltpu.VMEM
    out = jax.ShapeDtypeStruct
    scratch = [
        vmem((3, W, TOK), BF16),
        vmem((4 * W, 640), BF16),
        vmem((TOK, 640), BF16),
        vmem((8, 2, WP, TOK), BF16),
        vmem((256, WP), BF16),
        vmem((WP, 256), BF16),
        vmem((256, WP), BF16),
        vmem((WP, 256), BF16),
        vmem((256, WP), F32),
        vmem((256, 1), F32),
        vmem((256, 1), F32),
        vmem((256, WP), F32),
        vmem((8, 2, WR, TOK), F32),
        vmem((4, TOK, WP), BF16),
        vmem((4, TOK, WP), BF16),
        vmem((8, 48, WP), BF16),
        vmem((8, 48, WP), BF16),
        vmem((8, 32, WP), BF16),
        vmem((8, 16, WP), BF16),
        vmem((8, 16, WP), BF16),
        vmem((8, 16, WP), F32),
        vmem((8, 16, WP), F32),
        vmem((8, 16, TOK), F32),
        vmem((8, 16, TOK), F32),
        vmem((8, 48, WP), BF16),
        vmem((8, 48, WP), BF16),
        vmem((8, 32, WP), BF16),
        vmem((8, 32, WP), BF16),
        vmem((4, 32, WP), BF16),
        vmem((4, 32, WP), BF16),
        vmem((4, TOK, WP), BF16),
        vmem((2, 320, TOK), BF16),
        vmem((8, 320, TOK), BF16),
        vmem((8, TOK, WP), BF16),
        vmem((4, 80, WP), BF16),
        vmem((4, 80, WP), BF16),
        vmem((4, 32, WP), BF16),
        vmem((4, 32, WP), BF16),
        vmem((4, 8, WP), F32),
        vmem((4, 8, WP), F32),
        vmem((8, 2, WR, TOK), BF16),
        vmem((8, 2, WR, TOK), BF16),
        vmem((TOK, TOK), F32),
        vmem((TOK, WP), F32),
    ]
    sems = [dma((5,))] + [dma((8, 2))] * 4 + [dma((4,))] * 4 + [dma((8,))] * 14 + [dma((2,))] * 2 + [dma((4,))] * 2 + [dma((8,))] * 4 + [dma((4,))] * 6
    shapes = (
        out((TOK, 640), BF16),
        out((W, TOK), BF16),
        out((W, TOK), BF16),
        out((W, TOK), BF16),
        out((5, 4 * W), F32),
    )
    outs = pl.pallas_call(
        kernel,
        out_shape=shapes,
        in_specs=[hbm] * 5,
        out_specs=[vm] * 5,
        scratch_shapes=scratch + sems,
        compiler_params=pltpu.CompilerParams(
            collective_id=0, has_side_effects=True, vmem_limit_bytes=62 * 2**20
        ),
    )(queries.T, keys.T, values.T, weight_out.T, grad_out)
    lay, gq, gk, gv, gw = pl.pallas_call(
        hand_over, out_shape=shapes, in_specs=[vm] * 5, out_specs=[vm] * 5
    )(*outs)
    return lay, gq.T, gk.T, gv.T, gw


def solution(mesh):
    placed = (P("seq", "mp"), P("seq", "mp"), P("seq", "mp"), P("mp", None), P("seq", "mp"))
    return jax.shard_map(
        body,
        mesh=mesh,
        in_specs=placed,
        out_specs=(
            P("seq", "mp"),
            P("seq", "mp"),
            P("seq", "mp"),
            P("seq", "mp"),
            P(("mp", "seq"), None),
        ),
        check_vma=False,
    )
```

```python
import jax
import jax.numpy as jnp
from jax import lax
from jax.experimental import pallas as pl
from jax.experimental.pallas import tpu as pltpu
from jax.sharding import PartitionSpec as P

MESH = pl.DeviceIdType.MESH
HD = 150
VIA_OUT = 0
VIA_BACK = 4
W = 300
WP = 384
WR = 304
TOK = 128
NEG = -1e30
SCALE = HD ** (-0.5)
F32 = jnp.float32
BF16 = jnp.bfloat16


def nn(a, b):
    return jnp.dot(a, b, preferred_element_type=F32)


def nt(a, b):
    return lax.dot_general(a, b, (((1,), (1,)), ((), ())), preferred_element_type=F32)


def tn(a, b):
    return lax.dot_general(a, b, (((0,), (0,)), ((), ())), preferred_element_type=F32)


def iota(shape, dim):
    return lax.broadcasted_iota(jnp.int32, shape, dim)


def head_pair(x):
    lane = iota(x.shape, 1)
    a = jnp.where(lane < HD, x, 0.0)
    b = jnp.where((lane >= HD) & (lane < W), x, 0.0)
    return jnp.concatenate([a, b], axis=0).astype(BF16)


def head_columns(x):
    row = iota(x.shape, 0)
    a = jnp.where(row < HD, x, 0.0)
    b = jnp.where((row >= HD) & (row < W), x, 0.0)
    return jnp.concatenate([a, b], axis=1).astype(BF16)


def pick(x2):
    n = x2.shape[0] // 2
    lane = iota((n, WP), 1)
    return jnp.where(lane < HD, x2[:n], x2[n:])


def each(n, f):
    lax.fori_loop(1, n, lambda i, c: (f(i), c)[1], 0)


class Exchange:
    def __init__(self, n, out, into):
        self.n, self.out, self.into = n, out, into

    def start(self):
        each(self.n, lambda i: self.out(i).start())

    def arrive(self):
        each(self.n, lambda i: self.into(i).wait_recv())

    def sent(self):
        each(self.n, lambda i: self.out(i).wait_send())


def kernel(
    q_hbm, k_hbm, v_hbm, w_hbm, go_hbm,
    lay_ref, gq_ref, gk_ref, gv_ref, gw_ref,
    xin, w_ref, go_ref, kv, q2, q2t, d2, d2t, acc2, m_ref, l_ref, gq2, own,
    part, mpin, cola, colain, colxin, cold, coldin, colo, coloin, coli, coliin,
    colg, colgin, colh, colhin, viax, viah,
    att, goh, goin, gwin, gz1, z1in, gz2, z2in, gfx, fxin, rbs, rbin, info, dat,
    in_s, row_s, row_r, rb_s, rb_r, mp_s, mp_r, ag_s, ag_r,
    ca_s, ca_r, cx_s, cx_r, cd_s, cd_r, co_s, co_r, ci_s, ci_r, cg_s, cg_r, ch_s, ch_r, hop_s, hop_r, vx_s, vh_s,
    go_s, go_r, gw_s, gw_r, z1_s, z1_r, z2_s, z2_r, fx_s, fx_r,
):
    s = lax.axis_index("seq")
    m = lax.axis_index("mp")
    cg = s % 8
    yh, x, z = s // 64, (s // 16) % 4, s % 16
    zq, zr = z // 4, z % 4
    g = yh * 4 + x

    def copy(src, dst, ss, rs, dev):
        return pltpu.make_async_remote_copy(
            src_ref=src, dst_ref=dst, send_sem=ss, recv_sem=rs, device_id=dev, device_id_type=MESH
        )

    def exchange(n, me, dev, src, dst, ss, rs):
        def other(i):
            return (me + i) % n

        def out(i):
            o = other(i)
            return copy(src(o), dst.at[me], ss.at[o], rs.at[me], dev(o))

        def into(i):
            o = other(i)
            return copy(src(o), dst.at[o], ss.at[o], rs.at[o], dev(o))

        return Exchange(n, out, into)

    def g_dev(o):
        return ((o // 4) * 64 + (o % 4) * 16 + z, m)

    def z_dev(o):
        return (yh * 64 + x * 16 + o, m)

    def mp_dev(o):
        return (s, o)

    def columns(src, dst, ss, rs):
        return exchange(8, g, g_dev, lambda o: src.at[o], dst, ss, rs)

    def far_dev(o, d):
        return ((o // 4) * 64 + (o % 4) * 16 + (z + 16 + d) % 16, m)

    class Across:
        def __init__(self, n, src, dst, via, d, ss, rs, vs, k):
            self.n, self.first = n, 8 - n
            self.src, self.dst, self.via, self.d, self.ss, self.rs, self.vs, self.k = src, dst, via, d, ss, rs, vs, k

        def hop(self):
            return copy(self.src(pl.ds(self.first, self.n)), self.via.at[pl.ds(0, self.n)], hop_s.at[self.k], hop_r.at[self.k], far_dev(g, self.d))

        def straight(self, o):
            return copy(self.src(o), self.dst.at[g], self.ss.at[o], self.rs.at[g], far_dev(o, 8))

        def onward(self, o):
            return copy(self.via.at[o], self.dst.at[g], self.vs.at[o], self.rs.at[g], far_dev(o + self.first, 7 * self.d))

        def start(self):
            if self.n:
                self.hop().start()
            lax.fori_loop(0, self.first, lambda o, c: (self.straight(o).start(), c)[1], 0)

        def relay(self):
            if self.n:
                self.hop().wait_recv()
                lax.fori_loop(0, self.n, lambda o, c: (self.onward(o).start(), c)[1], 0)

        def arrive(self):
            def one(o, c):
                copy(self.src(o), self.dst.at[o], self.ss.at[o], self.rs.at[o], far_dev(o, 8)).wait_recv()
                return c

            lax.fori_loop(0, 8, one, 0)

        def sent(self):
            lax.fori_loop(0, self.first, lambda o, c: (self.straight(o).wait_send(), c)[1], 0)
            if self.n:
                self.hop().wait_send()
                lax.fori_loop(0, self.n, lambda o, c: (self.onward(o).wait_send(), c)[1], 0)

    ex_mp = exchange(4, m, mp_dev, lambda o: part.at[o], mpin, mp_s, mp_r)
    ex_ag = exchange(4, m, mp_dev, lambda o: att.at[m], att, ag_s, ag_r)
    ex_ca = columns(cola, colain, ca_s, ca_r)
    ex_cx = Across(VIA_OUT, lambda o: cola.at[o, pl.ds(16, 32)], colxin, viax, -1, cx_s, cx_r, vx_s, 0)
    ex_cd = columns(cold, coldin, cd_s, cd_r)
    ex_co = columns(colo, coloin, co_s, co_r)
    ex_ci = columns(coli, coliin, ci_s, ci_r)
    ex_cg = columns(colg, colgin, cg_s, cg_r)
    ex_ch = Across(VIA_BACK, lambda o: colh.at[o], colhin, viah, 1, ch_s, ch_r, vh_s, 1)
    ex_go = exchange(8, g, g_dev, lambda o: goh.at[o // 4], goin, go_s, go_r)

    def gw_target(j):
        return ((j // 4) * 64 + (m + 4 - j % 4) % 4 * 16 + z, j % 4)

    def gw_source(o):
        return ((o // 4) * 64 + (o % 4) * 16 + z, (x + m) % 4)

    def gw_mine(j):
        return (x == 0) & (j // 4 == yh) & (j % 4 == m)

    def gw_out(j):
        return copy(att.at[m], gwin.at[g, pl.ds(0, WR)], gw_s.at[j], gw_r.at[g], gw_target(j))

    def gw_into(o):
        return copy(att.at[m], gwin.at[o, pl.ds(0, WR)], gw_s.at[o], gw_r.at[o], gw_source(o))

    def over8(skip, f):
        def one(i, c):
            @pl.when(jnp.logical_not(skip(i)))
            def _():
                f(i)

            return c

        lax.fori_loop(0, 8, one, 0)

    ex_z1 = exchange(4, zr, lambda o: z_dev(zq * 4 + o), lambda o: gz1.at[o], z1in, z1_s, z1_r)
    ex_z2 = exchange(4, zq, lambda o: z_dev(o * 4 + zr), lambda o: gz2.at[o], z2in, z2_s, z2_r)
    ex_fx = exchange(4, x, lambda o: (yh * 64 + o * 16 + z, m), lambda o: gfx.at[o], fxin, fx_s, fx_r)

    loads = [
        pltpu.make_async_copy(a, b, in_s.at[i])
        for i, (a, b) in enumerate(
            (
                (q_hbm, xin.at[0]), (k_hbm, xin.at[1]), (v_hbm, xin.at[2]),
                (go_hbm, go_ref), (w_hbm, w_ref),
            )
        )
    ]
    for c in loads:
        c.start()
    kv[:, :, 288:, :] = jnp.zeros((8, 2, WP - 288, TOK), BF16)
    gwin[:, WR:, :] = jnp.zeros((8, WP - WR, TOK), BF16)
    bar = pltpu.get_barrier_semaphore()

    def greet(dev):
        pl.semaphore_signal(bar, inc=1, device_id=dev, device_id_type=MESH)

    each(8, lambda i: greet(g_dev((g + i) % 8)))

    straight = 8 - min(VIA_OUT, VIA_BACK)

    def greet_sender(o, c):
        @pl.when(g < straight)
        def _():
            greet(far_dev(o, 8))

        for n, d in ((VIA_OUT, 7), (VIA_BACK, -7)):
            @pl.when(g >= 8 - n)
            def _(d=d):
                greet(far_dev(o, d))

        return c

    lax.fori_loop(0, 8, greet_sender, 0)
    greet(far_dev(g, 1))
    greet(far_dev(g, -1))
    over8(lambda o: (x == 0) & (o == g), lambda o: greet(gw_source(o)))
    each(4, lambda i: greet((s, (m + i) % 4)))
    each(4, lambda i: greet(z_dev(zq * 4 + (zr + i) % 4)))
    each(4, lambda i: greet(z_dev(((zq + i) % 4) * 4 + zr)))

    @pl.when(cg > 0)
    def _():
        greet((s - 1, m))

    @pl.when(cg < 7)
    def _():
        greet((s + 1, m))

    for c in loads[:3]:
        c.wait()
    kv[0, 0, :W, :] = xin[1]
    kv[0, 1, :W, :] = xin[2]
    fill = jnp.zeros((WP - W, TOK), F32)
    qt = jnp.concatenate([xin[0].astype(F32), fill], axis=0)
    q2t[...] = head_columns(qt)
    q32 = qt.T
    k32 = kv[0, 0].astype(F32).T
    v32 = kv[0, 1].astype(F32).T
    q2[...] = head_pair(q32)
    for i, t in enumerate((q32, k32, v32)):
        cola[:, 16 * i : 16 * i + 16, :] = t.astype(BF16).reshape(8, 16, WP)
    for c in loads[3:]:
        c.wait()
    pg = nt(go_ref[...], w_ref[...])
    lanes = jnp.zeros((TOK, WP - W), F32)
    for i in range(4):
        part[i] = jnp.concatenate([pg[:, W * i : W * i + W], lanes], axis=1).astype(BF16)
    go_t = go_ref[...].astype(F32).T.astype(BF16)
    goh[0] = go_t[:320]
    goh[1] = go_t[320:]

    links = (cg > 0).astype(jnp.int32) + (cg < 7).astype(jnp.int32)
    pl.semaphore_wait(bar, 7 + straight + VIA_OUT + VIA_BACK + 2 + 8 + 3 + 3 + 3 + links - (x == 0).astype(jnp.int32))

    def row_copy(t, i):
        return copy(
            kv.at[t, i, pl.ds(0, WR)], kv.at[t + 1, i, pl.ds(0, WR)],
            row_s.at[t, i], row_r.at[t + 1, i], (s + 1, m),
        )

    def row_arrival(t, i):
        return copy(
            kv.at[t, i, pl.ds(0, WR)], kv.at[t, i, pl.ds(0, WR)],
            row_s.at[t, i], row_r.at[t, i], (s - 1, m),
        )

    @pl.when(cg < 7)
    def _():
        row_copy(0, 0).start()
        row_copy(0, 1).start()

    ex_cx.start()
    ex_mp.start()
    ex_ca.start()
    colain[g] = cola[g]
    ex_go.start()
    goin[g] = goh[yh]

    def scores(t):
        return nn(q2[...], kv[t, 0]) * SCALE

    def row_first():
        sc = scores(0)
        ok = iota((256, TOK), 0) % TOK >= iota((256, TOK), 1)
        sc = jnp.where(ok, sc, NEG)
        mx = jnp.max(sc, axis=1, keepdims=True)
        p = jnp.exp(sc - mx)
        m_ref[...] = mx
        l_ref[...] = jnp.sum(p, axis=1, keepdims=True)
        acc2[...] = nt(p.astype(BF16), kv[0, 1])

    def row_step(t):
        @pl.when(cg >= t)
        def _():
            for i in range(2):
                row_arrival(t, i).wait_recv()

                @pl.when(cg < 7)
                def _():
                    row_copy(t, i).start()

            sc = scores(t)
            old = m_ref[...]
            mx = jnp.maximum(old, jnp.max(sc, axis=1, keepdims=True))
            p = jnp.exp(sc - mx)
            w = jnp.exp(old - mx)
            m_ref[...] = mx
            l_ref[...] = l_ref[...] * w + jnp.sum(p, axis=1, keepdims=True)
            acc2[...] = acc2[...] * w + nt(p.astype(BF16), kv[t, 1])

    def row_steps(lo, hi):
        lax.fori_loop(lo, hi, lambda t, c: (row_step(t), c)[1], 0)

    def finish_dattn():
        ex_mp.arrive()
        d = part[m].astype(F32)
        for i in range(1, 4):
            d = d + mpin[(m + i) % 4].astype(F32)
        d = d.astype(BF16).astype(F32)
        dat[...] = d
        d2[...] = head_pair(d)
        d2t[...] = head_columns(d.T)
        cold[...] = d.astype(BF16).reshape(8, 16, WP)
        ex_cd.start()
        coldin[g] = cold[g]

    def column_rows(ref, i):
        return ref[:, 16 * i : 16 * i + 16, :].reshape(TOK, WP)

    def column_operands():
        ck = jnp.concatenate([column_rows(colain, 1), column_rows(colxin, 0)], axis=0)
        cv = jnp.concatenate([column_rows(colain, 2), column_rows(colxin, 1)], axis=0)
        return head_pair(column_rows(colain, 0).astype(F32)), ck, cv

    def column_mask(shape, qdim):
        qi = iota(shape, qdim) % TOK
        kj = iota(shape, 1 - qdim)
        ki = kj % TOK
        later = jnp.where(kj < TOK, 0, z // 8)
        return (qi % 16 == ki % 16) & (ki // 16 < qi // 16 + later)

    def col_forward():
        ex_ca.arrive()
        ex_cx.arrive()
        cq2, ck, cv = column_operands()
        sc = nt(cq2, ck) * SCALE
        ok = column_mask((256, 256), 0)
        mx = jnp.max(jnp.where(ok, sc, NEG), axis=1, keepdims=True)
        p = jnp.where(ok, jnp.exp(sc - mx), 0.0)
        tot = jnp.sum(p, axis=1, keepdims=True)
        some = tot > 0.0
        safe = jnp.where(some, tot, 1.0)
        o = pick(nn(p.astype(BF16), cv) / safe)
        lse = jnp.where(some, mx + jnp.log(safe), NEG)
        lane = iota((TOK, WP), 1)
        o = jnp.where(lane < W, o, jnp.where(lane < 340, lse[:TOK], lse[TOK:]))
        colo[...] = o.reshape(8, 16, WP)
        ex_co.start()
        coloin[g] = colo[g]

    def merge():
        ex_co.arrive()
        far = coloin[...].reshape(TOK, WP)
        lane = iota((TOK, WP), 1)
        d = dat[...]
        near = pick(acc2[...])
        lses, near_w, far_w = [], [], []
        for h in range(2):
            lo = W + 40 * h
            here = (lane >= lo) & (lane < lo + 40)
            fl = jnp.max(jnp.where(here, far, -3e38), axis=1, keepdims=True)
            mr = m_ref[h * TOK : h * TOK + TOK, :]
            nl = mr + jnp.log(l_ref[h * TOK : h * TOK + TOK, :])
            top = jnp.maximum(nl, fl)
            lse = top + jnp.log(jnp.exp(nl - top) + jnp.exp(fl - top))
            lses.append(lse)
            near_w.append(jnp.exp(mr - lse))
            far_w.append(jnp.exp(fl - lse))
        nw = jnp.where(lane < HD, near_w[0], near_w[1])
        fw = jnp.where(lane < HD, far_w[0], far_w[1])
        a = jnp.where(lane < W, near * nw + far * fw, 0.0).astype(BF16)
        att[m] = a.astype(F32).T[:WR].astype(BF16)
        over8(gw_mine, lambda j: gw_out(j).start())

        @pl.when(x == 0)
        def _():
            gwin[g, 0:WR] = att[m]

        prod = a.astype(F32) * d
        d0 = jnp.sum(jnp.where(lane < HD, prod, 0.0), axis=1, keepdims=True)
        d1 = jnp.sum(jnp.where((lane >= HD) & (lane < W), prod, 0.0), axis=1, keepdims=True)
        ln = iota((TOK, TOK), 1)
        both = jnp.where(ln < 64, jnp.where(ln < 32, lses[0], lses[1]), jnp.where(ln < 96, d0, d1))
        coli[...] = both.reshape(8, 16, TOK)
        ex_ci.start()
        coliin[g] = coli[g]
        ex_ag.start()
        info[...] = both
        gq2[...] = jnp.zeros_like(gq2)

    def stats(a):
        pair = [jnp.concatenate([a[:, i : i + 1], a[:, i + 32 : i + 33]], axis=0) for i in (0, 64)]
        return pair[0], pair[1]

    def row_own(u):
        @pl.when(cg >= u)
        def _():
            t = cg - u
            lse, delta = stats(info[...])
            k_t, v_t = kv[t, 0], kv[t, 1]
            ok = (t > 0) | (iota((256, TOK), 0) % TOK >= iota((256, TOK), 1))
            p = jnp.where(ok, jnp.exp(scores(t) - lse), 0.0)
            dp = nn(d2[...], v_t)
            ds = (p * (dp - delta)).astype(BF16)
            own[u, 0] = (nn(q2t[...], ds) * SCALE)[:WR]
            own[u, 1] = nn(d2t[...], p.astype(BF16))[:WR]
            gq2[...] += nt(ds, k_t)

    def rb_copy(u, i):
        return copy(rbs.at[u, i], rbin.at[u, i], rb_s.at[u, i], rb_r.at[u, i], (s - 1, m))

    def row_chain(u):
        @pl.when(cg >= u)
        def _():
            for i in range(2):
                @pl.when(cg < 7)
                def _():
                    rb_copy(u, i).wait_recv()
                    own[u, i] += rbin[u, i].astype(F32)

                @pl.when(cg > u)
                def _():
                    rbs[u, i] = own[u, i].astype(BF16)
                    rb_copy(u, i).start()

    def layer():
        ex_ag.arrive()
        full = jnp.concatenate([att[i].astype(F32).T[:, :W] for i in range(4)], axis=1).astype(BF16)
        lay_ref[...] = nn(full, w_ref[...]).astype(BF16)

    def gw_product():
        ex_go.arrive()
        over8(lambda o: (x == 0) & (o == g), lambda o: gw_into(o).wait_recv())
        prod = nt(goin[0], gwin[0])
        for i in range(1, 8):
            prod = prod + nt(goin[i], gwin[i])
        to = iota((320, 320), 0)
        src = ((to // 5 % 4) * 16 + (to // 20 % 4) * 4 + to // 80) * 5 + to % 5
        perm = (src == iota((320, 320), 1)).astype(F32).astype(BF16)
        gz1[...] = nn(perm, prod.astype(BF16)).astype(BF16).reshape(4, 80, WP)
        ex_z1.start()

    def gw_level1():
        ex_z1.arrive()
        t = gz1[zr].astype(F32)
        for i in range(1, 4):
            t = t + z1in[(zr + i) % 4].astype(F32)
        to = iota((TOK, 80), 0)
        src = jnp.where(to % 8 < 5, to // 8 * 5 + to % 8, -1)
        perm = (src == iota((TOK, 80), 1)).astype(F32).astype(BF16)
        gz2[...] = nn(perm, t.astype(BF16)).astype(BF16).reshape(4, 32, WP)
        ex_z2.start()

    def gw_level2():
        ex_z2.arrive()
        t = gz2[zq].astype(F32)
        for i in range(1, 4):
            t = t + z2in[(zq + i) % 4].astype(F32)
        gfx[...] = t.reshape(4, 8, WP)
        ex_fx.start()
        fxin[x] = gfx[x]

    def gw_finish():
        ex_fx.arrive()
        gw_ref[...] = jnp.concatenate([fxin[(i + 4 - m) % 4][:, :W] for i in range(4)], axis=1)[:5]

    def col_backward():
        ex_ci.arrive()
        ex_cd.arrive()
        cq2, ck, cv = column_operands()
        cd2 = head_pair(coldin[...].reshape(TOK, WP).astype(F32))
        both = coliin[...].reshape(TOK, TOK).T
        lse = jnp.concatenate([both[0:1], both[32:33]], axis=1)
        delta = jnp.concatenate([both[64:65], both[96:97]], axis=1)
        sc = nt(ck, cq2) * SCALE
        ok = column_mask((256, 256), 1)
        p = jnp.where(ok, jnp.exp(sc - lse), 0.0)
        dp = nt(cv, cd2)
        ds = (p * (dp - delta)).astype(BF16)
        ggk = nn(ds, cq2) * SCALE
        ggv = nn(p.astype(BF16), cd2)
        ggq = pick(tn(ds, ck)) * SCALE
        for i, t in enumerate((ggk, ggv)):
            colh[:, 16 * i : 16 * i + 16, :] = t[TOK:].astype(BF16).reshape(8, 16, WP)
        ex_ch.start()
        for i, t in enumerate((ggq, ggk[:TOK], ggv[:TOK])):
            colg[:, 16 * i : 16 * i + 16, :] = t.astype(BF16).reshape(8, 16, WP)
        ex_cg.start()
        colgin[g] = colg[g]

    def both(u):
        row_own(u)
        row_chain(u)

    def results():
        ex_cg.arrive()
        ex_ch.arrive()
        hq, hk, hv = (column_rows(colgin, i).astype(F32) for i in range(3))
        hk = hk + column_rows(colhin, 0).astype(F32)
        hv = hv + column_rows(colhin, 1).astype(F32)
        gq_ref[...] = (pick(gq2[...]) * SCALE + hq).T[:W].astype(BF16)
        gk_ref[...] = (own[cg, 0] + hk.T[:WR])[:W].astype(BF16)
        gv_ref[...] = (own[cg, 1] + hv.T[:WR])[:W].astype(BF16)

    def tick(u):
        row_own(u)

        @pl.when(u + cg >= 7)
        def _():
            row_chain(u + cg - 7)

    def ticks(lo, hi):
        lax.fori_loop(lo, hi, lambda u, c: (tick(u), c)[1], 0)

    row_first()
    ex_cx.relay()
    finish_dattn()
    row_steps(1, 3)
    col_forward()
    row_steps(3, 8)
    merge()
    ticks(0, 2)
    col_backward()
    ticks(2, 3)
    gw_product()
    ex_ch.relay()
    ticks(3, 5)
    gw_level1()
    ticks(5, 7)
    layer()
    gw_level2()
    ticks(7, 8)
    results()
    gw_finish()

    def sent(t, c):
        @pl.when((cg < 7) & (t <= cg))
        def _():
            row_copy(t, 0).wait_send()
            row_copy(t, 1).wait_send()

        @pl.when(t < cg)
        def _():
            rb_copy(t, 0).wait_send()
            rb_copy(t, 1).wait_send()

        return c

    lax.fori_loop(0, 8, sent, 0)
    for e in (ex_mp, ex_ag, ex_ca, ex_cx, ex_cd, ex_co, ex_ci, ex_cg, ex_ch, ex_go, ex_z1, ex_z2, ex_fx):
        e.sent()
    over8(gw_mine, lambda j: gw_out(j).wait_send())


def hand_over(*refs):
    for a, b in zip(refs[:5], refs[5:]):
        b[...] = a[...]


def body(queries, keys, values, weight_out, grad_out):
    vm = pl.BlockSpec(memory_space=pltpu.VMEM)
    hbm = pl.BlockSpec(memory_space=pltpu.HBM)
    dma = pltpu.SemaphoreType.DMA
    vmem = pltpu.VMEM
    out = jax.ShapeDtypeStruct
    scratch = [
        vmem((3, W, TOK), BF16),
        vmem((4 * W, 640), BF16),
        vmem((TOK, 640), BF16),
        vmem((8, 2, WP, TOK), BF16),
        vmem((256, WP), BF16),
        vmem((WP, 256), BF16),
        vmem((256, WP), BF16),
        vmem((WP, 256), BF16),
        vmem((256, WP), F32),
        vmem((256, 1), F32),
        vmem((256, 1), F32),
        vmem((256, WP), F32),
        vmem((8, 2, WR, TOK), F32),
        vmem((4, TOK, WP), BF16),
        vmem((4, TOK, WP), BF16),
        vmem((8, 48, WP), BF16),
        vmem((8, 48, WP), BF16),
        vmem((8, 32, WP), BF16),
        vmem((8, 16, WP), BF16),
        vmem((8, 16, WP), BF16),
        vmem((8, 16, WP), F32),
        vmem((8, 16, WP), F32),
        vmem((8, 16, TOK), F32),
        vmem((8, 16, TOK), F32),
        vmem((8, 48, WP), BF16),
        vmem((8, 48, WP), BF16),
        vmem((8, 32, WP), BF16),
        vmem((8, 32, WP), BF16),
        vmem((8, 32, WP), BF16),
        vmem((8, 32, WP), BF16),
        vmem((4, WR, TOK), BF16),
        vmem((2, 320, TOK), BF16),
        vmem((8, 320, TOK), BF16),
        vmem((8, WP, TOK), BF16),
        vmem((4, 80, WP), BF16),
        vmem((4, 80, WP), BF16),
        vmem((4, 32, WP), BF16),
        vmem((4, 32, WP), BF16),
        vmem((4, 8, WP), F32),
        vmem((4, 8, WP), F32),
        vmem((8, 2, WR, TOK), BF16),
        vmem((8, 2, WR, TOK), BF16),
        vmem((TOK, TOK), F32),
        vmem((TOK, WP), F32),
    ]
    sems = [dma((5,))] + [dma((8, 2))] * 4 + [dma((4,))] * 4 + [dma((8,))] * 14 + [dma((2,))] * 2 + [dma((8,))] * 6 + [dma((4,))] * 6
    shapes = (
        out((TOK, 640), BF16),
        out((W, TOK), BF16),
        out((W, TOK), BF16),
        out((W, TOK), BF16),
        out((5, 4 * W), F32),
    )
    outs = pl.pallas_call(
        kernel,
        out_shape=shapes,
        in_specs=[hbm] * 5,
        out_specs=[vm] * 5,
        scratch_shapes=scratch + sems,
        compiler_params=pltpu.CompilerParams(
            collective_id=0, has_side_effects=True, vmem_limit_bytes=62 * 2**20
        ),
    )(queries.T, keys.T, values.T, weight_out.T, grad_out)
    lay, gq, gk, gv, gw = pl.pallas_call(
        hand_over, out_shape=shapes, in_specs=[vm] * 5, out_specs=[vm] * 5
    )(*outs)
    return lay, gq.T, gk.T, gv.T, gw


def solution(mesh):
    placed = (P("seq", "mp"), P("seq", "mp"), P("seq", "mp"), P("mp", None), P("seq", "mp"))
    return jax.shard_map(
        body,
        mesh=mesh,
        in_specs=placed,
        out_specs=(
            P("seq", "mp"),
            P("seq", "mp"),
            P("seq", "mp"),
            P("seq", "mp"),
            P(("mp", "seq"), None),
        ),
        check_vma=False,
    )
```

```python
import jax
import jax.numpy as jnp
from jax import lax
from jax.experimental import pallas as pl
from jax.experimental.pallas import tpu as pltpu
from jax.sharding import PartitionSpec as P

MESH = pl.DeviceIdType.MESH
HD = 150
VIA_OUT = 1
VIA_BACK = 4
W = 300
WP = 384
WR = 304
TOK = 128
NEG = -1e30
SCALE = HD ** (-0.5)
F32 = jnp.float32
BF16 = jnp.bfloat16


def nn(a, b):
    return jnp.dot(a, b, preferred_element_type=F32)


def nt(a, b):
    return lax.dot_general(a, b, (((1,), (1,)), ((), ())), preferred_element_type=F32)


def tn(a, b):
    return lax.dot_general(a, b, (((0,), (0,)), ((), ())), preferred_element_type=F32)


def iota(shape, dim):
    return lax.broadcasted_iota(jnp.int32, shape, dim)


def head_pair(x):
    lane = iota(x.shape, 1)
    a = jnp.where(lane < HD, x, 0.0)
    b = jnp.where((lane >= HD) & (lane < W), x, 0.0)
    return jnp.concatenate([a, b], axis=0).astype(BF16)


def head_columns(x):
    row = iota(x.shape, 0)
    a = jnp.where(row < HD, x, 0.0)
    b = jnp.where((row >= HD) & (row < W), x, 0.0)
    return jnp.concatenate([a, b], axis=1).astype(BF16)


def pick(x2):
    n = x2.shape[0] // 2
    lane = iota((n, WP), 1)
    return jnp.where(lane < HD, x2[:n], x2[n:])


def two_in_one(a, b):
    rest = a[:, 256:] + pltpu.roll(b[:, 256:], 64, 1)
    return jnp.concatenate([a[:, :256], b[:, :256], rest], axis=1).astype(BF16)


def one_in_two(x):
    x = x.astype(F32)
    rest = x[:, 512:]
    low = iota(rest.shape, 1) < 64
    a = jnp.concatenate([x[:, :256], jnp.where(low, rest, 0.0)], axis=1)
    b = jnp.concatenate([x[:, 256:512], jnp.where(low, pltpu.roll(rest, 64, 1), 0.0)], axis=1)
    return a, b


def each(n, f):
    lax.fori_loop(1, n, lambda i, c: (f(i), c)[1], 0)


class Exchange:
    def __init__(self, n, out, into):
        self.n, self.out, self.into = n, out, into

    def start(self):
        each(self.n, lambda i: self.out(i).start())

    def arrive(self):
        each(self.n, lambda i: self.into(i).wait_recv())

    def sent(self):
        each(self.n, lambda i: self.out(i).wait_send())


def kernel(
    q_hbm, k_hbm, v_hbm, w_hbm, go_hbm,
    lay_ref, gq_ref, gk_ref, gv_ref, gw_ref,
    xin, w_ref, go_ref, kv, q2, q2t, d2, d2t, acc2, m_ref, l_ref, gq2, own,
    part, mpin, cola, colain, colx, colxin, cold, coldin, colo, coloin, coli, coliin,
    colg, colgin, colh, colhin, viax, viah,
    att, goh, goin, gwin, gz1, z1in, gz2, z2in, gfx, fxin, rbs, rbin, info, dat,
    in_s, row_s, row_r, rb_s, rb_r, mp_s, mp_r, ag_s, ag_r,
    ca_s, ca_r, cx_s, cx_r, cd_s, cd_r, co_s, co_r, ci_s, ci_r, cg_s, cg_r, ch_s, ch_r, hop_s, hop_r, vx_s, vh_s,
    go_s, go_r, gw_s, gw_r, z1_s, z1_r, z2_s, z2_r, fx_s, fx_r,
):
    s = lax.axis_index("seq")
    m = lax.axis_index("mp")
    cg = s % 8
    yh, x, z = s // 64, (s // 16) % 4, s % 16
    zq, zr = z // 4, z % 4
    g = yh * 4 + x

    def copy(src, dst, ss, rs, dev):
        return pltpu.make_async_remote_copy(
            src_ref=src, dst_ref=dst, send_sem=ss, recv_sem=rs, device_id=dev, device_id_type=MESH
        )

    def exchange(n, me, dev, src, dst, ss, rs):
        def other(i):
            return (me + i) % n

        def out(i):
            o = other(i)
            return copy(src(o), dst.at[me], ss.at[o], rs.at[me], dev(o))

        def into(i):
            o = other(i)
            return copy(src(o), dst.at[o], ss.at[o], rs.at[o], dev(o))

        return Exchange(n, out, into)

    def g_dev(o):
        return ((o // 4) * 64 + (o % 4) * 16 + z, m)

    def z_dev(o):
        return (yh * 64 + x * 16 + o, m)

    def mp_dev(o):
        return (s, o)

    def columns(src, dst, ss, rs):
        return exchange(8, g, g_dev, lambda o: src.at[o], dst, ss, rs)

    def far_dev(o, d):
        return ((o // 4) * 64 + (o % 4) * 16 + (z + 16 + d) % 16, m)

    class Across:
        def __init__(self, n, src, dst, via, d, ss, rs, vs, k):
            self.n, self.first = n, 8 - n
            self.src, self.dst, self.via, self.d, self.ss, self.rs, self.vs, self.k = src, dst, via, d, ss, rs, vs, k

        def hop(self):
            return copy(self.src(pl.ds(self.first, self.n)), self.via.at[pl.ds(0, self.n)], hop_s.at[self.k], hop_r.at[self.k], far_dev(g, self.d))

        def straight(self, o):
            return copy(self.src(o), self.dst.at[g], self.ss.at[o], self.rs.at[g], far_dev(o, 8))

        def onward(self, o):
            return copy(self.via.at[o], self.dst.at[g], self.vs.at[o], self.rs.at[g], far_dev(o + self.first, 7 * self.d))

        def start(self):
            if self.n:
                self.hop().start()
            lax.fori_loop(0, self.first, lambda o, c: (self.straight(o).start(), c)[1], 0)

        def relay(self):
            if self.n:
                self.hop().wait_recv()
                lax.fori_loop(0, self.n, lambda o, c: (self.onward(o).start(), c)[1], 0)

        def arrive(self):
            def one(o, c):
                copy(self.src(o), self.dst.at[o], self.ss.at[o], self.rs.at[o], far_dev(o, 8)).wait_recv()
                return c

            lax.fori_loop(0, 8, one, 0)

        def sent(self):
            lax.fori_loop(0, self.first, lambda o, c: (self.straight(o).wait_send(), c)[1], 0)
            if self.n:
                self.hop().wait_send()
                lax.fori_loop(0, self.n, lambda o, c: (self.onward(o).wait_send(), c)[1], 0)

    ex_mp = exchange(4, m, mp_dev, lambda o: part.at[o], mpin, mp_s, mp_r)
    ex_ag = exchange(4, m, mp_dev, lambda o: att.at[m], att, ag_s, ag_r)
    ex_ca = columns(cola, colain, ca_s, ca_r)
    ex_cx = Across(VIA_OUT, lambda o: colx.at[o], colxin, viax, -1, cx_s, cx_r, vx_s, 0)
    ex_cd = columns(cold, coldin, cd_s, cd_r)
    ex_co = columns(colo, coloin, co_s, co_r)
    ex_ci = columns(coli, coliin, ci_s, ci_r)
    ex_cg = columns(colg, colgin, cg_s, cg_r)
    ex_ch = Across(VIA_BACK, lambda o: colh.at[o], colhin, viah, 1, ch_s, ch_r, vh_s, 1)
    ex_go = exchange(8, g, g_dev, lambda o: goh.at[o // 4], goin, go_s, go_r)

    def gw_target(j):
        return ((j // 4) * 64 + (m + 4 - j % 4) % 4 * 16 + z, j % 4)

    def gw_source(o):
        return ((o // 4) * 64 + (o % 4) * 16 + z, (x + m) % 4)

    def gw_mine(j):
        return (x == 0) & (j // 4 == yh) & (j % 4 == m)

    def gw_out(j):
        return copy(att.at[m], gwin.at[g, pl.ds(0, WR)], gw_s.at[j], gw_r.at[g], gw_target(j))

    def gw_into(o):
        return copy(att.at[m], gwin.at[o, pl.ds(0, WR)], gw_s.at[o], gw_r.at[o], gw_source(o))

    def over8(skip, f):
        def one(i, c):
            @pl.when(jnp.logical_not(skip(i)))
            def _():
                f(i)

            return c

        lax.fori_loop(0, 8, one, 0)

    ex_z1 = exchange(4, zr, lambda o: z_dev(zq * 4 + o), lambda o: gz1.at[o], z1in, z1_s, z1_r)
    ex_z2 = exchange(4, zq, lambda o: z_dev(o * 4 + zr), lambda o: gz2.at[o], z2in, z2_s, z2_r)
    ex_fx = exchange(4, x, lambda o: (yh * 64 + o * 16 + z, m), lambda o: gfx.at[o], fxin, fx_s, fx_r)

    loads = [
        pltpu.make_async_copy(a, b, in_s.at[i])
        for i, (a, b) in enumerate(
            (
                (q_hbm, xin.at[0]), (k_hbm, xin.at[1]), (v_hbm, xin.at[2]),
                (go_hbm, go_ref), (w_hbm, w_ref),
            )
        )
    ]
    for c in loads:
        c.start()
    kv[:, :, 288:, :] = jnp.zeros((8, 2, WP - 288, TOK), BF16)
    gwin[:, WR:, :] = jnp.zeros((8, WP - WR, TOK), BF16)
    bar = pltpu.get_barrier_semaphore()

    def greet(dev):
        pl.semaphore_signal(bar, inc=1, device_id=dev, device_id_type=MESH)

    each(8, lambda i: greet(g_dev((g + i) % 8)))

    straight = 8 - min(VIA_OUT, VIA_BACK)

    def greet_sender(o, c):
        @pl.when(g < straight)
        def _():
            greet(far_dev(o, 8))

        for n, d in ((VIA_OUT, 7), (VIA_BACK, -7)):
            @pl.when(g >= 8 - n)
            def _(d=d):
                greet(far_dev(o, d))

        return c

    lax.fori_loop(0, 8, greet_sender, 0)
    greet(far_dev(g, 1))
    greet(far_dev(g, -1))
    over8(lambda o: (x == 0) & (o == g), lambda o: greet(gw_source(o)))
    each(4, lambda i: greet((s, (m + i) % 4)))
    each(4, lambda i: greet(z_dev(zq * 4 + (zr + i) % 4)))
    each(4, lambda i: greet(z_dev(((zq + i) % 4) * 4 + zr)))

    @pl.when(cg > 0)
    def _():
        greet((s - 1, m))

    @pl.when(cg < 7)
    def _():
        greet((s + 1, m))

    for c in loads[:3]:
        c.wait()
    kv[0, 0, :W, :] = xin[1]
    kv[0, 1, :W, :] = xin[2]
    fill = jnp.zeros((WP - W, TOK), F32)
    qt = jnp.concatenate([xin[0].astype(F32), fill], axis=0)
    q2t[...] = head_columns(qt)
    q32 = qt.T
    k32 = kv[0, 0].astype(F32).T
    v32 = kv[0, 1].astype(F32).T
    q2[...] = head_pair(q32)
    for i, t in enumerate((q32, k32, v32)):
        cola[:, 16 * i : 16 * i + 16, :] = t.astype(BF16).reshape(8, 16, WP)
    colx[...] = two_in_one(k32, v32).reshape(8, 16, 640)
    for c in loads[3:]:
        c.wait()
    pg = nt(go_ref[...], w_ref[...])
    lanes = jnp.zeros((TOK, WP - W), F32)
    for i in range(4):
        part[i] = jnp.concatenate([pg[:, W * i : W * i + W], lanes], axis=1).astype(BF16)
    go_t = go_ref[...].astype(F32).T.astype(BF16)
    goh[0] = go_t[:320]
    goh[1] = go_t[320:]

    links = (cg > 0).astype(jnp.int32) + (cg < 7).astype(jnp.int32)
    pl.semaphore_wait(bar, 7 + straight + VIA_OUT + VIA_BACK + 2 + 8 + 3 + 3 + 3 + links - (x == 0).astype(jnp.int32))

    def row_copy(t, i):
        return copy(
            kv.at[t, i, pl.ds(0, WR)], kv.at[t + 1, i, pl.ds(0, WR)],
            row_s.at[t, i], row_r.at[t + 1, i], (s + 1, m),
        )

    def row_arrival(t, i):
        return copy(
            kv.at[t, i, pl.ds(0, WR)], kv.at[t, i, pl.ds(0, WR)],
            row_s.at[t, i], row_r.at[t, i], (s - 1, m),
        )

    @pl.when(cg < 7)
    def _():
        row_copy(0, 0).start()
        row_copy(0, 1).start()

    ex_cx.start()
    ex_mp.start()
    ex_ca.start()
    colain[g] = cola[g]

    def scores(t):
        return nn(q2[...], kv[t, 0]) * SCALE

    def row_first():
        sc = scores(0)
        ok = iota((256, TOK), 0) % TOK >= iota((256, TOK), 1)
        sc = jnp.where(ok, sc, NEG)
        mx = jnp.max(sc, axis=1, keepdims=True)
        p = jnp.exp(sc - mx)
        m_ref[...] = mx
        l_ref[...] = jnp.sum(p, axis=1, keepdims=True)
        acc2[...] = nt(p.astype(BF16), kv[0, 1])

    def row_step(t):
        @pl.when(cg >= t)
        def _():
            for i in range(2):
                row_arrival(t, i).wait_recv()

                @pl.when(cg < 7)
                def _():
                    row_copy(t, i).start()

            sc = scores(t)
            old = m_ref[...]
            mx = jnp.maximum(old, jnp.max(sc, axis=1, keepdims=True))
            p = jnp.exp(sc - mx)
            w = jnp.exp(old - mx)
            m_ref[...] = mx
            l_ref[...] = l_ref[...] * w + jnp.sum(p, axis=1, keepdims=True)
            acc2[...] = acc2[...] * w + nt(p.astype(BF16), kv[t, 1])

    def row_steps(lo, hi):
        lax.fori_loop(lo, hi, lambda t, c: (row_step(t), c)[1], 0)

    def finish_dattn():
        ex_mp.arrive()
        d = part[m].astype(F32)
        for i in range(1, 4):
            d = d + mpin[(m + i) % 4].astype(F32)
        d = d.astype(BF16).astype(F32)
        dat[...] = d
        d2[...] = head_pair(d)
        d2t[...] = head_columns(d.T)
        cold[...] = d.astype(BF16).reshape(8, 16, WP)
        ex_cd.start()
        coldin[g] = cold[g]

    def column_rows(ref, i):
        return ref[:, 16 * i : 16 * i + 16, :].reshape(TOK, WP)

    def column_operands():
        fk, fv = one_in_two(colxin[...].reshape(TOK, 640))
        ck = jnp.concatenate([column_rows(colain, 1), fk.astype(BF16)], axis=0)
        cv = jnp.concatenate([column_rows(colain, 2), fv.astype(BF16)], axis=0)
        return head_pair(column_rows(colain, 0).astype(F32)), ck, cv

    def column_mask(shape, qdim):
        qi = iota(shape, qdim) % TOK
        kj = iota(shape, 1 - qdim)
        ki = kj % TOK
        later = jnp.where(kj < TOK, 0, z // 8)
        return (qi % 16 == ki % 16) & (ki // 16 < qi // 16 + later)

    def col_forward():
        ex_ca.arrive()
        ex_cx.arrive()
        cq2, ck, cv = column_operands()
        sc = nt(cq2, ck) * SCALE
        ok = column_mask((256, 256), 0)
        mx = jnp.max(jnp.where(ok, sc, NEG), axis=1, keepdims=True)
        p = jnp.where(ok, jnp.exp(sc - mx), 0.0)
        tot = jnp.sum(p, axis=1, keepdims=True)
        some = tot > 0.0
        safe = jnp.where(some, tot, 1.0)
        o = pick(nn(p.astype(BF16), cv) / safe)
        lse = jnp.where(some, mx + jnp.log(safe), NEG)
        lane = iota((TOK, WP), 1)
        o = jnp.where(lane < W, o, jnp.where(lane < 340, lse[:TOK], lse[TOK:]))
        colo[...] = o.reshape(8, 16, WP)
        ex_co.start()
        coloin[g] = colo[g]

    def merge():
        ex_co.arrive()
        far = coloin[...].reshape(TOK, WP)
        lane = iota((TOK, WP), 1)
        d = dat[...]
        near = pick(acc2[...])
        lses, near_w, far_w = [], [], []
        for h in range(2):
            lo = W + 40 * h
            here = (lane >= lo) & (lane < lo + 40)
            fl = jnp.max(jnp.where(here, far, -3e38), axis=1, keepdims=True)
            mr = m_ref[h * TOK : h * TOK + TOK, :]
            nl = mr + jnp.log(l_ref[h * TOK : h * TOK + TOK, :])
            top = jnp.maximum(nl, fl)
            lse = top + jnp.log(jnp.exp(nl - top) + jnp.exp(fl - top))
            lses.append(lse)
            near_w.append(jnp.exp(mr - lse))
            far_w.append(jnp.exp(fl - lse))
        nw = jnp.where(lane < HD, near_w[0], near_w[1])
        fw = jnp.where(lane < HD, far_w[0], far_w[1])
        a = jnp.where(lane < W, near * nw + far * fw, 0.0).astype(BF16)
        att[m] = a.astype(F32).T[:WR].astype(BF16)
        over8(gw_mine, lambda j: gw_out(j).start())

        @pl.when(x == 0)
        def _():
            gwin[g, 0:WR] = att[m]

        prod = a.astype(F32) * d
        d0 = jnp.sum(jnp.where(lane < HD, prod, 0.0), axis=1, keepdims=True)
        d1 = jnp.sum(jnp.where((lane >= HD) & (lane < W), prod, 0.0), axis=1, keepdims=True)
        ln = iota((TOK, TOK), 1)
        both = jnp.where(ln < 64, jnp.where(ln < 32, lses[0], lses[1]), jnp.where(ln < 96, d0, d1))
        coli[...] = both.reshape(8, 16, TOK)
        ex_ci.start()
        coliin[g] = coli[g]
        ex_ag.start()
        info[...] = both
        gq2[...] = jnp.zeros_like(gq2)

    def stats(a):
        pair = [jnp.concatenate([a[:, i : i + 1], a[:, i + 32 : i + 33]], axis=0) for i in (0, 64)]
        return pair[0], pair[1]

    def row_own(u):
        @pl.when(cg >= u)
        def _():
            t = cg - u
            lse, delta = stats(info[...])
            k_t, v_t = kv[t, 0], kv[t, 1]
            ok = (t > 0) | (iota((256, TOK), 0) % TOK >= iota((256, TOK), 1))
            p = jnp.where(ok, jnp.exp(scores(t) - lse), 0.0)
            dp = nn(d2[...], v_t)
            ds = (p * (dp - delta)).astype(BF16)
            own[u, 0] = (nn(q2t[...], ds) * SCALE)[:WR]
            own[u, 1] = nn(d2t[...], p.astype(BF16))[:WR]
            gq2[...] += nt(ds, k_t)

    def rb_copy(u, i):
        return copy(rbs.at[u, i], rbin.at[u, i], rb_s.at[u, i], rb_r.at[u, i], (s - 1, m))

    def row_chain(u):
        @pl.when(cg >= u)
        def _():
            for i in range(2):
                @pl.when(cg < 7)
                def _():
                    rb_copy(u, i).wait_recv()
                    own[u, i] += rbin[u, i].astype(F32)

                @pl.when(cg > u)
                def _():
                    rbs[u, i] = own[u, i].astype(BF16)
                    rb_copy(u, i).start()

    def layer():
        ex_ag.arrive()
        full = jnp.concatenate([att[i].astype(F32).T[:, :W] for i in range(4)], axis=1).astype(BF16)
        lay_ref[...] = nn(full, w_ref[...]).astype(BF16)

    def gw_product():
        ex_go.arrive()
        over8(lambda o: (x == 0) & (o == g), lambda o: gw_into(o).wait_recv())
        prod = nt(goin[0], gwin[0])
        for i in range(1, 8):
            prod = prod + nt(goin[i], gwin[i])
        to = iota((320, 320), 0)
        src = ((to // 5 % 4) * 16 + (to // 20 % 4) * 4 + to // 80) * 5 + to % 5
        perm = (src == iota((320, 320), 1)).astype(F32).astype(BF16)
        gz1[...] = nn(perm, prod.astype(BF16)).astype(BF16).reshape(4, 80, WP)
        ex_z1.start()

    def gw_level1():
        ex_z1.arrive()
        t = gz1[zr].astype(F32)
        for i in range(1, 4):
            t = t + z1in[(zr + i) % 4].astype(F32)
        to = iota((TOK, 80), 0)
        src = jnp.where(to % 8 < 5, to // 8 * 5 + to % 8, -1)
        perm = (src == iota((TOK, 80), 1)).astype(F32).astype(BF16)
        gz2[...] = nn(perm, t.astype(BF16)).astype(BF16).reshape(4, 32, WP)
        ex_z2.start()

    def gw_level2():
        ex_z2.arrive()
        t = gz2[zq].astype(F32)
        for i in range(1, 4):
            t = t + z2in[(zq + i) % 4].astype(F32)
        gfx[...] = t.reshape(4, 8, WP)
        ex_fx.start()
        fxin[x] = gfx[x]

    def gw_finish():
        ex_fx.arrive()
        gw_ref[...] = jnp.concatenate([fxin[(i + 4 - m) % 4][:, :W] for i in range(4)], axis=1)[:5]

    def col_backward():
        ex_ci.arrive()
        ex_cd.arrive()
        cq2, ck, cv = column_operands()
        cd2 = head_pair(coldin[...].reshape(TOK, WP).astype(F32))
        both = coliin[...].reshape(TOK, TOK).T
        lse = jnp.concatenate([both[0:1], both[32:33]], axis=1)
        delta = jnp.concatenate([both[64:65], both[96:97]], axis=1)
        sc = nt(ck, cq2) * SCALE
        ok = column_mask((256, 256), 1)
        p = jnp.where(ok, jnp.exp(sc - lse), 0.0)
        dp = nt(cv, cd2)
        ds = (p * (dp - delta)).astype(BF16)
        ggk = nn(ds, cq2) * SCALE
        ggv = nn(p.astype(BF16), cd2)
        ggq = pick(tn(ds, ck)) * SCALE
        colh[...] = two_in_one(ggk[TOK:], ggv[TOK:]).reshape(8, 16, 640)
        ex_ch.start()
        for i, t in enumerate((ggq, ggk[:TOK], ggv[:TOK])):
            colg[:, 16 * i : 16 * i + 16, :] = t.astype(BF16).reshape(8, 16, WP)
        ex_cg.start()
        colgin[g] = colg[g]

    def both(u):
        row_own(u)
        row_chain(u)

    def results():
        ex_cg.arrive()
        ex_ch.arrive()
        hq, hk, hv = (column_rows(colgin, i).astype(F32) for i in range(3))
        fk, fv = one_in_two(colhin[...].reshape(TOK, 640))
        hk = hk + fk
        hv = hv + fv
        gq_ref[...] = (pick(gq2[...]) * SCALE + hq).T[:W].astype(BF16)
        gk_ref[...] = (own[cg, 0] + hk.T[:WR])[:W].astype(BF16)
        gv_ref[...] = (own[cg, 1] + hv.T[:WR])[:W].astype(BF16)

    def tick(u):
        row_own(u)

        @pl.when(u + cg >= 7)
        def _():
            row_chain(u + cg - 7)

    def ticks(lo, hi):
        lax.fori_loop(lo, hi, lambda u, c: (tick(u), c)[1], 0)

    row_first()
    ex_cx.relay()
    finish_dattn()
    ex_go.start()
    goin[g] = goh[yh]
    row_steps(1, 4)
    col_forward()
    row_steps(4, 8)
    merge()
    ticks(0, 2)
    col_backward()
    ticks(2, 3)
    gw_product()
    ex_ch.relay()
    ticks(3, 5)
    gw_level1()
    ticks(5, 7)
    layer()
    gw_level2()
    ticks(7, 8)
    results()
    gw_finish()

    def sent(t, c):
        @pl.when((cg < 7) & (t <= cg))
        def _():
            row_copy(t, 0).wait_send()
            row_copy(t, 1).wait_send()

        @pl.when(t < cg)
        def _():
            rb_copy(t, 0).wait_send()
            rb_copy(t, 1).wait_send()

        return c

    lax.fori_loop(0, 8, sent, 0)
    for e in (ex_mp, ex_ag, ex_ca, ex_cx, ex_cd, ex_co, ex_ci, ex_cg, ex_ch, ex_go, ex_z1, ex_z2, ex_fx):
        e.sent()
    over8(gw_mine, lambda j: gw_out(j).wait_send())


def hand_over(*refs):
    for a, b in zip(refs[:5], refs[5:]):
        b[...] = a[...]


def body(queries, keys, values, weight_out, grad_out):
    vm = pl.BlockSpec(memory_space=pltpu.VMEM)
    hbm = pl.BlockSpec(memory_space=pltpu.HBM)
    dma = pltpu.SemaphoreType.DMA
    vmem = pltpu.VMEM
    out = jax.ShapeDtypeStruct
    scratch = [
        vmem((3, W, TOK), BF16),
        vmem((4 * W, 640), BF16),
        vmem((TOK, 640), BF16),
        vmem((8, 2, WP, TOK), BF16),
        vmem((256, WP), BF16),
        vmem((WP, 256), BF16),
        vmem((256, WP), BF16),
        vmem((WP, 256), BF16),
        vmem((256, WP), F32),
        vmem((256, 1), F32),
        vmem((256, 1), F32),
        vmem((256, WP), F32),
        vmem((8, 2, WR, TOK), F32),
        vmem((4, TOK, WP), BF16),
        vmem((4, TOK, WP), BF16),
        vmem((8, 48, WP), BF16),
        vmem((8, 48, WP), BF16),
        vmem((8, 16, 640), BF16),
        vmem((8, 16, 640), BF16),
        vmem((8, 16, WP), BF16),
        vmem((8, 16, WP), BF16),
        vmem((8, 16, WP), F32),
        vmem((8, 16, WP), F32),
        vmem((8, 16, TOK), F32),
        vmem((8, 16, TOK), F32),
        vmem((8, 48, WP), BF16),
        vmem((8, 48, WP), BF16),
        vmem((8, 16, 640), BF16),
        vmem((8, 16, 640), BF16),
        vmem((8, 16, 640), BF16),
        vmem((8, 16, 640), BF16),
        vmem((4, WR, TOK), BF16),
        vmem((2, 320, TOK), BF16),
        vmem((8, 320, TOK), BF16),
        vmem((8, WP, TOK), BF16),
        vmem((4, 80, WP), BF16),
        vmem((4, 80, WP), BF16),
        vmem((4, 32, WP), BF16),
        vmem((4, 32, WP), BF16),
        vmem((4, 8, WP), F32),
        vmem((4, 8, WP), F32),
        vmem((8, 2, WR, TOK), BF16),
        vmem((8, 2, WR, TOK), BF16),
        vmem((TOK, TOK), F32),
        vmem((TOK, WP), F32),
    ]
    sems = [dma((5,))] + [dma((8, 2))] * 4 + [dma((4,))] * 4 + [dma((8,))] * 14 + [dma((2,))] * 2 + [dma((8,))] * 6 + [dma((4,))] * 6
    shapes = (
        out((TOK, 640), BF16),
        out((W, TOK), BF16),
        out((W, TOK), BF16),
        out((W, TOK), BF16),
        out((5, 4 * W), F32),
    )
    outs = pl.pallas_call(
        kernel,
        out_shape=shapes,
        in_specs=[hbm] * 5,
        out_specs=[vm] * 5,
        scratch_shapes=scratch + sems,
        compiler_params=pltpu.CompilerParams(
            collective_id=0, has_side_effects=True, vmem_limit_bytes=62 * 2**20
        ),
    )(queries.T, keys.T, values.T, weight_out.T, grad_out)
    lay, gq, gk, gv, gw = pl.pallas_call(
        hand_over, out_shape=shapes, in_specs=[vm] * 5, out_specs=[vm] * 5
    )(*outs)
    return lay, gq.T, gk.T, gv.T, gw


def solution(mesh):
    placed = (P("seq", "mp"), P("seq", "mp"), P("seq", "mp"), P("mp", None), P("seq", "mp"))
    return jax.shard_map(
        body,
        mesh=mesh,
        in_specs=placed,
        out_specs=(
            P("seq", "mp"),
            P("seq", "mp"),
            P("seq", "mp"),
            P("seq", "mp"),
            P(("mp", "seq"), None),
        ),
        check_vma=False,
    )
```

```python
import jax
import jax.numpy as jnp
from jax import lax
from jax.experimental import pallas as pl
from jax.experimental.pallas import tpu as pltpu
from jax.sharding import PartitionSpec as P

MESH = pl.DeviceIdType.MESH
HD = 150
VIA_OUT = 1
VIA_BACK = 5
W = 300
WP = 384
WR = 304
TOK = 128
NEG = -1e30
SCALE = HD ** (-0.5)
F32 = jnp.float32
BF16 = jnp.bfloat16


def nn(a, b):
    return jnp.dot(a, b, preferred_element_type=F32)


def nt(a, b):
    return lax.dot_general(a, b, (((1,), (1,)), ((), ())), preferred_element_type=F32)


def tn(a, b):
    return lax.dot_general(a, b, (((0,), (0,)), ((), ())), preferred_element_type=F32)


def iota(shape, dim):
    return lax.broadcasted_iota(jnp.int32, shape, dim)


def head_pair(x):
    lane = iota(x.shape, 1)
    a = jnp.where(lane < HD, x, 0.0)
    b = jnp.where((lane >= HD) & (lane < W), x, 0.0)
    return jnp.concatenate([a, b], axis=0).astype(BF16)


def head_columns(x):
    row = iota(x.shape, 0)
    a = jnp.where(row < HD, x, 0.0)
    b = jnp.where((row >= HD) & (row < W), x, 0.0)
    return jnp.concatenate([a, b], axis=1).astype(BF16)


def pick(x2):
    n = x2.shape[0] // 2
    lane = iota((n, WP), 1)
    return jnp.where(lane < HD, x2[:n], x2[n:])


def two_in_one(a, b):
    rest = a[:, 256:] + pltpu.roll(b[:, 256:], 64, 1)
    return jnp.concatenate([a[:, :256], b[:, :256], rest], axis=1).astype(BF16)


def one_in_two(x):
    x = x.astype(F32)
    rest = x[:, 512:]
    low = iota(rest.shape, 1) < 64
    a = jnp.concatenate([x[:, :256], jnp.where(low, rest, 0.0)], axis=1)
    b = jnp.concatenate([x[:, 256:512], jnp.where(low, pltpu.roll(rest, 64, 1), 0.0)], axis=1)
    return a, b


def each(n, f):
    lax.fori_loop(1, n, lambda i, c: (f(i), c)[1], 0)


class Exchange:
    def __init__(self, n, out, into):
        self.n, self.out, self.into = n, out, into

    def start(self):
        each(self.n, lambda i: self.out(i).start())

    def arrive(self):
        each(self.n, lambda i: self.into(i).wait_recv())

    def sent(self):
        each(self.n, lambda i: self.out(i).wait_send())


def kernel(
    q_hbm, k_hbm, v_hbm, w_hbm, go_hbm,
    lay_ref, gq_ref, gk_ref, gv_ref, gw_ref,
    xin, w_ref, go_ref, kv, q2, q2t, d2, d2t, acc2, m_ref, l_ref, gq2, own,
    part, mpin, cola, colain, colx, colxin, cold, coldin, colo, coloin, coli, coliin,
    colg, colgin, colh, colhin, viax, viah,
    att, goh, goin, gwin, gz1, z1in, gz2, z2in, gfx, fxin, rbs, rbin, info, dat,
    in_s, row_s, row_r, rb_s, rb_r, mp_s, mp_r, ag_s, ag_r,
    ca_s, ca_r, cx_s, cx_r, cd_s, cd_r, co_s, co_r, ci_s, ci_r, cg_s, cg_r, ch_s, ch_r, hop_s, hop_r, vx_s, vh_s,
    go_s, go_r, gw_s, gw_r, z1_s, z1_r, z2_s, z2_r, fx_s, fx_r,
):
    s = lax.axis_index("seq")
    m = lax.axis_index("mp")
    cg = s % 8
    yh, x, z = s // 64, (s // 16) % 4, s % 16
    zq, zr = z // 4, z % 4
    g = yh * 4 + x

    def copy(src, dst, ss, rs, dev):
        return pltpu.make_async_remote_copy(
            src_ref=src, dst_ref=dst, send_sem=ss, recv_sem=rs, device_id=dev, device_id_type=MESH
        )

    def exchange(n, me, dev, src, dst, ss, rs):
        def other(i):
            return (me + i) % n

        def out(i):
            o = other(i)
            return copy(src(o), dst.at[me], ss.at[o], rs.at[me], dev(o))

        def into(i):
            o = other(i)
            return copy(src(o), dst.at[o], ss.at[o], rs.at[o], dev(o))

        return Exchange(n, out, into)

    def g_dev(o):
        return ((o // 4) * 64 + (o % 4) * 16 + z, m)

    def z_dev(o):
        return (yh * 64 + x * 16 + o, m)

    def mp_dev(o):
        return (s, o)

    def columns(src, dst, ss, rs):
        return exchange(8, g, g_dev, lambda o: src.at[o], dst, ss, rs)

    def far_dev(o, d):
        return ((o // 4) * 64 + (o % 4) * 16 + (z + 16 + d) % 16, m)

    class Across:
        def __init__(self, n, src, dst, via, d, ss, rs, vs, k):
            self.n, self.first = n, 8 - n
            self.src, self.dst, self.via, self.d, self.ss, self.rs, self.vs, self.k = src, dst, via, d, ss, rs, vs, k

        def hop(self):
            return copy(self.src(pl.ds(self.first, self.n)), self.via.at[pl.ds(0, self.n)], hop_s.at[self.k], hop_r.at[self.k], far_dev(g, self.d))

        def straight(self, o):
            return copy(self.src(o), self.dst.at[g], self.ss.at[o], self.rs.at[g], far_dev(o, 8))

        def onward(self, o):
            return copy(self.via.at[o], self.dst.at[g], self.vs.at[o], self.rs.at[g], far_dev(o + self.first, 7 * self.d))

        def start(self):
            if self.n:
                self.hop().start()
            lax.fori_loop(0, self.first, lambda o, c: (self.straight(o).start(), c)[1], 0)

        def relay(self):
            if self.n:
                self.hop().wait_recv()
                lax.fori_loop(0, self.n, lambda o, c: (self.onward(o).start(), c)[1], 0)

        def arrive(self):
            def one(o, c):
                copy(self.src(o), self.dst.at[o], self.ss.at[o], self.rs.at[o], far_dev(o, 8)).wait_recv()
                return c

            lax.fori_loop(0, 8, one, 0)

        def sent(self):
            lax.fori_loop(0, self.first, lambda o, c: (self.straight(o).wait_send(), c)[1], 0)
            if self.n:
                self.hop().wait_send()
                lax.fori_loop(0, self.n, lambda o, c: (self.onward(o).wait_send(), c)[1], 0)

    ex_mp = exchange(4, m, mp_dev, lambda o: part.at[o], mpin, mp_s, mp_r)
    ex_ag = exchange(4, m, mp_dev, lambda o: att.at[m], att, ag_s, ag_r)
    ex_ca = columns(cola, colain, ca_s, ca_r)
    ex_cx = Across(VIA_OUT, lambda o: colx.at[o], colxin, viax, -1, cx_s, cx_r, vx_s, 0)
    ex_cd = columns(cold, coldin, cd_s, cd_r)
    ex_co = columns(colo, coloin, co_s, co_r)
    ex_ci = columns(coli, coliin, ci_s, ci_r)
    ex_cg = columns(colg, colgin, cg_s, cg_r)
    ex_ch = Across(VIA_BACK, lambda o: colh.at[o], colhin, viah, 1, ch_s, ch_r, vh_s, 1)
    ex_go = exchange(8, g, g_dev, lambda o: goh.at[o // 4], goin, go_s, go_r)

    def gw_target(j):
        return ((j // 4) * 64 + (m + 4 - j % 4) % 4 * 16 + z, j % 4)

    def gw_source(o):
        return ((o // 4) * 64 + (o % 4) * 16 + z, (x + m) % 4)

    def gw_mine(j):
        return (x == 0) & (j // 4 == yh) & (j % 4 == m)

    def gw_out(j):
        return copy(att.at[m], gwin.at[g, pl.ds(0, WR)], gw_s.at[j], gw_r.at[g], gw_target(j))

    def gw_into(o):
        return copy(att.at[m], gwin.at[o, pl.ds(0, WR)], gw_s.at[o], gw_r.at[o], gw_source(o))

    def over8(skip, f):
        def one(i, c):
            @pl.when(jnp.logical_not(skip(i)))
            def _():
                f(i)

            return c

        lax.fori_loop(0, 8, one, 0)

    ex_z1 = exchange(4, zr, lambda o: z_dev(zq * 4 + o), lambda o: gz1.at[o], z1in, z1_s, z1_r)
    ex_z2 = exchange(4, zq, lambda o: z_dev(o * 4 + zr), lambda o: gz2.at[o], z2in, z2_s, z2_r)
    ex_fx = exchange(4, x, lambda o: (yh * 64 + o * 16 + z, m), lambda o: gfx.at[o], fxin, fx_s, fx_r)

    loads = [
        pltpu.make_async_copy(a, b, in_s.at[i])
        for i, (a, b) in enumerate(
            (
                (q_hbm, xin.at[0]), (k_hbm, xin.at[1]), (v_hbm, xin.at[2]),
                (go_hbm, go_ref), (w_hbm, w_ref),
            )
        )
    ]
    for c in loads:
        c.start()
    kv[:, :, 288:, :] = jnp.zeros((8, 2, WP - 288, TOK), BF16)
    gwin[:, WR:, :] = jnp.zeros((8, WP - WR, TOK), BF16)
    bar = pltpu.get_barrier_semaphore()

    def greet(dev):
        pl.semaphore_signal(bar, inc=1, device_id=dev, device_id_type=MESH)

    each(8, lambda i: greet(g_dev((g + i) % 8)))

    straight = 8 - min(VIA_OUT, VIA_BACK)

    def greet_sender(o, c):
        @pl.when(g < straight)
        def _():
            greet(far_dev(o, 8))

        for n, d in ((VIA_OUT, 7), (VIA_BACK, -7)):
            @pl.when(g >= 8 - n)
            def _(d=d):
                greet(far_dev(o, d))

        return c

    lax.fori_loop(0, 8, greet_sender, 0)
    greet(far_dev(g, 1))
    greet(far_dev(g, -1))
    over8(lambda o: (x == 0) & (o == g), lambda o: greet(gw_source(o)))
    each(4, lambda i: greet((s, (m + i) % 4)))
    each(4, lambda i: greet(z_dev(zq * 4 + (zr + i) % 4)))
    each(4, lambda i: greet(z_dev(((zq + i) % 4) * 4 + zr)))

    @pl.when(cg > 0)
    def _():
        greet((s - 1, m))

    @pl.when(cg < 7)
    def _():
        greet((s + 1, m))

    for c in loads[:3]:
        c.wait()
    kv[0, 0, :W, :] = xin[1]
    kv[0, 1, :W, :] = xin[2]
    fill = jnp.zeros((WP - W, TOK), F32)
    qt = jnp.concatenate([xin[0].astype(F32), fill], axis=0)
    q2t[...] = head_columns(qt)
    q32 = qt.T
    k32 = kv[0, 0].astype(F32).T
    v32 = kv[0, 1].astype(F32).T
    q2[...] = head_pair(q32)
    for i, t in enumerate((q32, k32, v32)):
        cola[:, 16 * i : 16 * i + 16, :] = t.astype(BF16).reshape(8, 16, WP)
    colx[...] = two_in_one(k32, v32).reshape(8, 16, 640)
    for c in loads[3:]:
        c.wait()
    pg = nt(go_ref[...], w_ref[...])
    lanes = jnp.zeros((TOK, WP - W), F32)
    for i in range(4):
        part[i] = jnp.concatenate([pg[:, W * i : W * i + W], lanes], axis=1).astype(BF16)
    go_t = go_ref[...].astype(F32).T.astype(BF16)
    goh[0] = go_t[:320]
    goh[1] = go_t[320:]

    links = (cg > 0).astype(jnp.int32) + (cg < 7).astype(jnp.int32)
    pl.semaphore_wait(bar, 7 + straight + VIA_OUT + VIA_BACK + 2 + 8 + 3 + 3 + 3 + links - (x == 0).astype(jnp.int32))

    def row_copy(t, i):
        return copy(
            kv.at[t, i, pl.ds(0, WR)], kv.at[t + 1, i, pl.ds(0, WR)],
            row_s.at[t, i], row_r.at[t + 1, i], (s + 1, m),
        )

    def row_arrival(t, i):
        return copy(
            kv.at[t, i, pl.ds(0, WR)], kv.at[t, i, pl.ds(0, WR)],
            row_s.at[t, i], row_r.at[t, i], (s - 1, m),
        )

    @pl.when(cg < 7)
    def _():
        row_copy(0, 0).start()
        row_copy(0, 1).start()

    ex_cx.start()
    ex_mp.start()
    ex_ca.start()
    colain[g] = cola[g]

    def scores(t):
        return nn(q2[...], kv[t, 0]) * SCALE

    def row_first():
        sc = scores(0)
        ok = iota((256, TOK), 0) % TOK >= iota((256, TOK), 1)
        sc = jnp.where(ok, sc, NEG)
        mx = jnp.max(sc, axis=1, keepdims=True)
        p = jnp.exp(sc - mx)
        m_ref[...] = mx
        l_ref[...] = jnp.sum(p, axis=1, keepdims=True)
        acc2[...] = nt(p.astype(BF16), kv[0, 1])

    def row_step(t):
        @pl.when(cg >= t)
        def _():
            for i in range(2):
                row_arrival(t, i).wait_recv()

                @pl.when(cg < 7)
                def _():
                    row_copy(t, i).start()

            sc = scores(t)
            old = m_ref[...]
            mx = jnp.maximum(old, jnp.max(sc, axis=1, keepdims=True))
            p = jnp.exp(sc - mx)
            w = jnp.exp(old - mx)
            m_ref[...] = mx
            l_ref[...] = l_ref[...] * w + jnp.sum(p, axis=1, keepdims=True)
            acc2[...] = acc2[...] * w + nt(p.astype(BF16), kv[t, 1])

    def row_steps(lo, hi):
        lax.fori_loop(lo, hi, lambda t, c: (row_step(t), c)[1], 0)

    def finish_dattn():
        ex_mp.arrive()
        d = part[m].astype(F32)
        for i in range(1, 4):
            d = d + mpin[(m + i) % 4].astype(F32)
        d = d.astype(BF16).astype(F32)
        dat[...] = d
        d2[...] = head_pair(d)
        d2t[...] = head_columns(d.T)
        cold[...] = d.astype(BF16).reshape(8, 16, WP)
        ex_cd.start()
        coldin[g] = cold[g]

    def column_rows(ref, i):
        return ref[:, 16 * i : 16 * i + 16, :].reshape(TOK, WP)

    def column_operands():
        fk, fv = one_in_two(colxin[...].reshape(TOK, 640))
        ck = jnp.concatenate([column_rows(colain, 1), fk.astype(BF16)], axis=0)
        cv = jnp.concatenate([column_rows(colain, 2), fv.astype(BF16)], axis=0)
        return head_pair(column_rows(colain, 0).astype(F32)), ck, cv

    def column_mask(shape, qdim):
        qi = iota(shape, qdim) % TOK
        kj = iota(shape, 1 - qdim)
        ki = kj % TOK
        later = jnp.where(kj < TOK, 0, z // 8)
        return (qi % 16 == ki % 16) & (ki // 16 < qi // 16 + later)

    def col_forward():
        ex_ca.arrive()
        ex_cx.arrive()
        cq2, ck, cv = column_operands()
        sc = nt(cq2, ck) * SCALE
        ok = column_mask((256, 256), 0)
        mx = jnp.max(jnp.where(ok, sc, NEG), axis=1, keepdims=True)
        p = jnp.where(ok, jnp.exp(sc - mx), 0.0)
        tot = jnp.sum(p, axis=1, keepdims=True)
        some = tot > 0.0
        safe = jnp.where(some, tot, 1.0)
        o = pick(nn(p.astype(BF16), cv) / safe)
        lse = jnp.where(some, mx + jnp.log(safe), NEG)
        lane = iota((TOK, WP), 1)
        o = jnp.where(lane < W, o, jnp.where(lane < 340, lse[:TOK], lse[TOK:]))
        colo[...] = o.reshape(8, 16, WP)
        ex_co.start()
        coloin[g] = colo[g]

    def merge():
        ex_co.arrive()
        far = coloin[...].reshape(TOK, WP)
        lane = iota((TOK, WP), 1)
        d = dat[...]
        near = pick(acc2[...])
        lses, near_w, far_w = [], [], []
        for h in range(2):
            lo = W + 40 * h
            here = (lane >= lo) & (lane < lo + 40)
            fl = jnp.max(jnp.where(here, far, -3e38), axis=1, keepdims=True)
            mr = m_ref[h * TOK : h * TOK + TOK, :]
            nl = mr + jnp.log(l_ref[h * TOK : h * TOK + TOK, :])
            top = jnp.maximum(nl, fl)
            lse = top + jnp.log(jnp.exp(nl - top) + jnp.exp(fl - top))
            lses.append(lse)
            near_w.append(jnp.exp(mr - lse))
            far_w.append(jnp.exp(fl - lse))
        nw = jnp.where(lane < HD, near_w[0], near_w[1])
        fw = jnp.where(lane < HD, far_w[0], far_w[1])
        a = jnp.where(lane < W, near * nw + far * fw, 0.0).astype(BF16)
        att[m] = a.astype(F32).T[:WR].astype(BF16)
        over8(gw_mine, lambda j: gw_out(j).start())

        @pl.when(x == 0)
        def _():
            gwin[g, 0:WR] = att[m]

        prod = a.astype(F32) * d
        d0 = jnp.sum(jnp.where(lane < HD, prod, 0.0), axis=1, keepdims=True)
        d1 = jnp.sum(jnp.where((lane >= HD) & (lane < W), prod, 0.0), axis=1, keepdims=True)
        ln = iota((TOK, TOK), 1)
        both = jnp.where(ln < 64, jnp.where(ln < 32, lses[0], lses[1]), jnp.where(ln < 96, d0, d1))
        coli[...] = both.reshape(8, 16, TOK)
        ex_ci.start()
        coliin[g] = coli[g]
        ex_ag.start()
        info[...] = both
        gq2[...] = jnp.zeros_like(gq2)

    def stats(a):
        pair = [jnp.concatenate([a[:, i : i + 1], a[:, i + 32 : i + 33]], axis=0) for i in (0, 64)]
        return pair[0], pair[1]

    def row_own(u):
        @pl.when(cg >= u)
        def _():
            t = cg - u
            lse, delta = stats(info[...])
            k_t, v_t = kv[t, 0], kv[t, 1]
            ok = (t > 0) | (iota((256, TOK), 0) % TOK >= iota((256, TOK), 1))
            p = jnp.where(ok, jnp.exp(scores(t) - lse), 0.0)
            dp = nn(d2[...], v_t)
            ds = (p * (dp - delta)).astype(BF16)
            own[u, 0] = (nn(q2t[...], ds) * SCALE)[:WR]
            own[u, 1] = nn(d2t[...], p.astype(BF16))[:WR]
            gq2[...] += nt(ds, k_t)

    def rb_copy(u, i):
        return copy(rbs.at[u, i], rbin.at[u, i], rb_s.at[u, i], rb_r.at[u, i], (s - 1, m))

    def row_chain(u):
        @pl.when(cg >= u)
        def _():
            for i in range(2):
                @pl.when(cg < 7)
                def _():
                    rb_copy(u, i).wait_recv()
                    own[u, i] += rbin[u, i].astype(F32)

                @pl.when(cg > u)
                def _():
                    rbs[u, i] = own[u, i].astype(BF16)
                    rb_copy(u, i).start()

    def layer():
        ex_ag.arrive()
        full = jnp.concatenate([att[i].astype(F32).T[:, :W] for i in range(4)], axis=1).astype(BF16)
        lay_ref[...] = nn(full, w_ref[...]).astype(BF16)

    def gw_product():
        ex_go.arrive()
        over8(lambda o: (x == 0) & (o == g), lambda o: gw_into(o).wait_recv())
        prod = nt(goin[0], gwin[0])
        for i in range(1, 8):
            prod = prod + nt(goin[i], gwin[i])
        to = iota((320, 320), 0)
        src = ((to // 5 % 4) * 16 + (to // 20 % 4) * 4 + to // 80) * 5 + to % 5
        perm = (src == iota((320, 320), 1)).astype(F32).astype(BF16)
        gz1[...] = nn(perm, prod.astype(BF16)).astype(BF16).reshape(4, 80, WP)
        ex_z1.start()

    def gw_level1():
        ex_z1.arrive()
        t = gz1[zr].astype(F32)
        for i in range(1, 4):
            t = t + z1in[(zr + i) % 4].astype(F32)
        to = iota((TOK, 80), 0)
        src = jnp.where(to % 8 < 5, to // 8 * 5 + to % 8, -1)
        perm = (src == iota((TOK, 80), 1)).astype(F32).astype(BF16)
        gz2[...] = nn(perm, t.astype(BF16)).astype(BF16).reshape(4, 32, WP)
        ex_z2.start()

    def gw_level2():
        ex_z2.arrive()
        t = gz2[zq].astype(F32)
        for i in range(1, 4):
            t = t + z2in[(zq + i) % 4].astype(F32)
        gfx[...] = t.reshape(4, 8, WP)
        ex_fx.start()
        fxin[x] = gfx[x]

    def gw_finish():
        ex_fx.arrive()
        gw_ref[...] = jnp.concatenate([fxin[(i + 4 - m) % 4][:, :W] for i in range(4)], axis=1)[:5]

    def col_backward():
        ex_ci.arrive()
        ex_cd.arrive()
        cq2, ck, cv = column_operands()
        cd2 = head_pair(coldin[...].reshape(TOK, WP).astype(F32))
        both = coliin[...].reshape(TOK, TOK).T
        lse = jnp.concatenate([both[0:1], both[32:33]], axis=1)
        delta = jnp.concatenate([both[64:65], both[96:97]], axis=1)
        sc = nt(ck, cq2) * SCALE
        ok = column_mask((256, 256), 1)
        p = jnp.where(ok, jnp.exp(sc - lse), 0.0)
        dp = nt(cv, cd2)
        ds = (p * (dp - delta)).astype(BF16)
        ggk = nn(ds, cq2) * SCALE
        ggv = nn(p.astype(BF16), cd2)
        ggq = pick(tn(ds, ck)) * SCALE
        colh[...] = two_in_one(ggk[TOK:], ggv[TOK:]).reshape(8, 16, 640)
        ex_ch.start()
        for i, t in enumerate((ggq, ggk[:TOK], ggv[:TOK])):
            colg[:, 16 * i : 16 * i + 16, :] = t.astype(BF16).reshape(8, 16, WP)
        ex_cg.start()
        colgin[g] = colg[g]

    def both(u):
        row_own(u)
        row_chain(u)

    def results():
        ex_cg.arrive()
        ex_ch.arrive()
        hq, hk, hv = (column_rows(colgin, i).astype(F32) for i in range(3))
        fk, fv = one_in_two(colhin[...].reshape(TOK, 640))
        hk = hk + fk
        hv = hv + fv
        gq_ref[...] = (pick(gq2[...]) * SCALE + hq).T[:W].astype(BF16)
        gk_ref[...] = (own[cg, 0] + hk.T[:WR])[:W].astype(BF16)
        gv_ref[...] = (own[cg, 1] + hv.T[:WR])[:W].astype(BF16)

    def tick(u):
        row_own(u)

        @pl.when(u + cg >= 7)
        def _():
            row_chain(u + cg - 7)

    def ticks(lo, hi):
        lax.fori_loop(lo, hi, lambda u, c: (tick(u), c)[1], 0)

    row_first()
    ex_cx.relay()
    finish_dattn()
    ex_go.start()
    goin[g] = goh[yh]
    row_steps(1, 4)
    col_forward()
    row_steps(4, 8)
    merge()
    ticks(0, 2)
    col_backward()
    ticks(2, 3)
    gw_product()
    ex_ch.relay()
    ticks(3, 5)
    gw_level1()
    ticks(5, 7)
    layer()
    gw_level2()
    ticks(7, 8)
    results()
    gw_finish()

    def sent(t, c):
        @pl.when((cg < 7) & (t <= cg))
        def _():
            row_copy(t, 0).wait_send()
            row_copy(t, 1).wait_send()

        @pl.when(t < cg)
        def _():
            rb_copy(t, 0).wait_send()
            rb_copy(t, 1).wait_send()

        return c

    lax.fori_loop(0, 8, sent, 0)
    for e in (ex_mp, ex_ag, ex_ca, ex_cx, ex_cd, ex_co, ex_ci, ex_cg, ex_ch, ex_go, ex_z1, ex_z2, ex_fx):
        e.sent()
    over8(gw_mine, lambda j: gw_out(j).wait_send())


def hand_over(*refs):
    for a, b in zip(refs[:5], refs[5:]):
        b[...] = a[...]


def body(queries, keys, values, weight_out, grad_out):
    vm = pl.BlockSpec(memory_space=pltpu.VMEM)
    hbm = pl.BlockSpec(memory_space=pltpu.HBM)
    dma = pltpu.SemaphoreType.DMA
    vmem = pltpu.VMEM
    out = jax.ShapeDtypeStruct
    scratch = [
        vmem((3, W, TOK), BF16),
        vmem((4 * W, 640), BF16),
        vmem((TOK, 640), BF16),
        vmem((8, 2, WP, TOK), BF16),
        vmem((256, WP), BF16),
        vmem((WP, 256), BF16),
        vmem((256, WP), BF16),
        vmem((WP, 256), BF16),
        vmem((256, WP), F32),
        vmem((256, 1), F32),
        vmem((256, 1), F32),
        vmem((256, WP), F32),
        vmem((8, 2, WR, TOK), F32),
        vmem((4, TOK, WP), BF16),
        vmem((4, TOK, WP), BF16),
        vmem((8, 48, WP), BF16),
        vmem((8, 48, WP), BF16),
        vmem((8, 16, 640), BF16),
        vmem((8, 16, 640), BF16),
        vmem((8, 16, WP), BF16),
        vmem((8, 16, WP), BF16),
        vmem((8, 16, WP), F32),
        vmem((8, 16, WP), F32),
        vmem((8, 16, TOK), F32),
        vmem((8, 16, TOK), F32),
        vmem((8, 48, WP), BF16),
        vmem((8, 48, WP), BF16),
        vmem((8, 16, 640), BF16),
        vmem((8, 16, 640), BF16),
        vmem((8, 16, 640), BF16),
        vmem((8, 16, 640), BF16),
        vmem((4, WR, TOK), BF16),
        vmem((2, 320, TOK), BF16),
        vmem((8, 320, TOK), BF16),
        vmem((8, WP, TOK), BF16),
        vmem((4, 80, WP), BF16),
        vmem((4, 80, WP), BF16),
        vmem((4, 32, WP), BF16),
        vmem((4, 32, WP), BF16),
        vmem((4, 8, WP), F32),
        vmem((4, 8, WP), F32),
        vmem((8, 2, WR, TOK), BF16),
        vmem((8, 2, WR, TOK), BF16),
        vmem((TOK, TOK), F32),
        vmem((TOK, WP), F32),
    ]
    sems = [dma((5,))] + [dma((8, 2))] * 4 + [dma((4,))] * 4 + [dma((8,))] * 14 + [dma((2,))] * 2 + [dma((8,))] * 6 + [dma((4,))] * 6
    shapes = (
        out((TOK, 640), BF16),
        out((W, TOK), BF16),
        out((W, TOK), BF16),
        out((W, TOK), BF16),
        out((5, 4 * W), F32),
    )
    outs = pl.pallas_call(
        kernel,
        out_shape=shapes,
        in_specs=[hbm] * 5,
        out_specs=[vm] * 5,
        scratch_shapes=scratch + sems,
        compiler_params=pltpu.CompilerParams(
            collective_id=0, has_side_effects=True, vmem_limit_bytes=62 * 2**20
        ),
    )(queries.T, keys.T, values.T, weight_out.T, grad_out)
    lay, gq, gk, gv, gw = pl.pallas_call(
        hand_over, out_shape=shapes, in_specs=[vm] * 5, out_specs=[vm] * 5
    )(*outs)
    return lay, gq.T, gk.T, gv.T, gw


def solution(mesh):
    placed = (P("seq", "mp"), P("seq", "mp"), P("seq", "mp"), P("mp", None), P("seq", "mp"))
    return jax.shard_map(
        body,
        mesh=mesh,
        in_specs=placed,
        out_specs=(
            P("seq", "mp"),
            P("seq", "mp"),
            P("seq", "mp"),
            P("seq", "mp"),
            P(("mp", "seq"), None),
        ),
        check_vma=False,
    )
```
